256 devices in a mesh: patch: 32 (over y, z), batch: 8 (over x, core).
Axes of the slice: x: 4, y: 4, z: 8, core: 2. Of those that a mesh axis runs over, the one named last changes fastest.
Arguments:
- hidden_in: bfloat16 [32768, 1536], P(('batch', 'patch')), parts along dimension 0, may hold values from -6 to 6
- queries: bfloat16 [32768, 768], P(('batch', 'patch')), parts along dimension 0, may hold values from -40 to 40
- fresh_kv: bfloat16 [32768, 1536], P(('batch', 'patch')), parts along dimension 0, may hold values from -144 to 144
- stale_kv: bfloat16 [32768, 1536], P(('batch', 'patch')), parts along dimension 0, may hold values from -144 to 144
- modulation: float32 [16, 1536], P('batch'), parts along dimension 0, may hold values from -3 to 3
- w_out: bfloat16 [768, 1536], replicated, may hold values from -0.21875 to 0.21875
- router: float32 [1536, 16], replicated, may hold values from -0.15625 to 0.15625
- fc_in: bfloat16 [32, 1536, 1536], P('patch'), may hold values from -0.15625 to 0.15625
- fc_out: bfloat16 [32, 1536, 1536], P('patch'), may hold values from -0.109375 to 0.109375
- expert_ids: int32 [32768, 2], P(('batch', 'patch')), parts along dimension 0, may hold values from 0 to 15, all different within a row; in each aligned block of 128 rows (0 to 127, 128 to 255, ...) at most 32 rows name the same one
Outputs:
- attended: bfloat16 [32768, 768], P(('batch', 'patch')), parts along dimension 0
- mixed: bfloat16 [32768, 1536], P(('batch', 'patch')), parts along dimension 0
The draws below stay inside these ranges and needn't reach their ends.
There are 8 independent parts, one for each index of `batch`. The reference program is written for one: setup_inputs(seed, part) draws one part's arguments, and reference() takes and returns one part's arrays. A program takes and returns all parts, laid end to end along the dimension named above; an argument that names none is the same for every part. Nothing has to cross between parts.
Inputs may be any that keep to these rules, and one draw needn't show every extreme that they name: `expert_ids`: within each aligned block of 128 rows (the rows of one index of patch) no expert is named more than 32 times; the two experts of a row differ.
All inputs are finite; a program needn't handle non-finite values.
Results may differ from the reference program's by a relative error of at most 0.007.
Values may be sent and summed in bfloat16 or wider, within the bound.
No kernel may reach another device: no remote copies, remote signals or barrier semaphores. Data moves between devices by JAX's collectives and lax.ppermute only.
A program may use at most 128 MiB of HBM per device.

```python
import math
import jax
import jax.numpy as jnp
import numpy as np
from jax import lax

D = 1536
HEADS = 8
HEAD = 96
FF = 3072
TOK_DEV = 128
HD = 768
EXPERTS = 16
TOKENS = 4096
CAP = 32
N_PATCH = 32


def draw_queries(key, part):
    key = jax.random.fold_in(key, 11)
    out = jax.random.truncated_normal(key, -6.0, 6.0, (TOKENS, HEADS * HEAD), jnp.float32)
    return out.astype(jnp.bfloat16)


def draw_fresh_kv(key, part):
    key = jax.random.fold_in(key, 23)
    key_a, key_b = jax.random.split(key)
    keys = jax.random.truncated_normal(key_a, -6.0, 6.0, (TOKENS, HEADS * HEAD), jnp.float32)
    values = 24.0 * jax.random.truncated_normal(key_b, -6.0, 6.0, (TOKENS, HEADS * HEAD), jnp.float32)
    return jnp.concatenate([keys, values], axis=1).astype(jnp.bfloat16)


def draw_stale_kv(key, part):
    key = jax.random.fold_in(key, 37)
    key_a, key_b = jax.random.split(key)
    keys = jax.random.truncated_normal(key_a, -6.0, 6.0, (TOKENS, HEADS * HEAD), jnp.float32)
    values = 24.0 * jax.random.truncated_normal(key_b, -6.0, 6.0, (TOKENS, HEADS * HEAD), jnp.float32)
    return jnp.concatenate([keys, values], axis=1).astype(jnp.bfloat16)


def levels(key, extent, shards, least, high):
    level, own = 1.0, jax.random.fold_in(key, 6)
    for dim, blocks in shards:
        steps = jnp.exp(jax.random.uniform(jax.random.fold_in(own, dim), (blocks,), jnp.float32, least / len(shards), high / len(shards)))
        level = level * jnp.repeat(steps, extent[dim] // blocks).reshape([-1 if axis == dim else 1 for axis in range(len(extent))])
    return level


def assign_block(key, own, number, rows, amount, top, limit, lean):
    ranking = jax.random.permutation(key, amount)
    heavy_load, usual = portions_of(amount, rows * top, limit, lean, True), portions_of(amount, rows * top, limit, lean, False)
    places = jnp.arange(amount)

    def named(lengths, turn):
        used = int((lengths > 0).sum())
        fixed = max(1, used // 4)
        shifted = fixed + (places - fixed + turn * (used - fixed)) % max(1, amount - fixed)
        return jnp.zeros((amount,), jnp.int32).at[ranking[jnp.where(places < fixed, places, shifted)]].set(jnp.asarray(lengths, jnp.int32))

    lengths = jnp.where(number % 4 == 0, named(heavy_load, number // 4), named(usual, number - number // 4 - 1))
    mixed = jax.random.permutation(jax.random.fold_in(own, 3), amount)
    source_of, sink = mixed[0:amount // 2 * 2:2], mixed[1:amount // 2 * 2:2]
    margin = jnp.minimum(lengths[source_of] - 1, limit - lengths[sink]) // 2
    margin = jnp.where((source_of == ranking[0]) | (sink == ranking[0]) | (lengths[sink] == 0), 0, jnp.maximum(margin, 0))
    shifted = jax.random.randint(jax.random.fold_in(own, 4), (amount // 2,), 0, 1 << 20) % (margin + 1)
    lengths = lengths.at[source_of].add(-shifted).at[sink].add(shifted)
    labels = jnp.searchsorted(jnp.cumsum(lengths), jnp.arange(rows * top), side="right").astype(jnp.int32)
    listing = labels.reshape(top, rows).T
    listing = listing[jax.random.permutation(jax.random.fold_in(own, 1), rows)]
    turn = jax.random.randint(jax.random.fold_in(own, 2), (rows, 1), 0, top)
    return jnp.take_along_axis(listing, (jnp.arange(top)[None, :] + turn) % top, axis=1)


def portions_of(count, total, reach, slope, full):
    portions = [(1 << 20) // math.isqrt(grade ** slope) + 1 for grade in range(1, count + 1)]
    largest = reach if full else min(reach, max(-(-total // count), total * portions[0] // sum(portions)))
    least = 1 if total - largest >= count - 1 else 0
    given, rest = [largest] + [least] * (count - 1), total - largest - least * (count - 1)
    while rest > 0:
        candidates = [i for i in range(1, count) if given[i] < largest] or [i for i in range(1, count) if given[i] < reach]
        pool, remaining = sum([portions[i] for i in candidates]), rest
        for i in candidates:
            extra = min(reach - given[i], max(1, remaining * portions[i] // pool), rest)
            given[i] = given[i] + extra
            rest = rest - extra
    return np.array(given)


def normal_values(stream_key, dims, deviation, bound, pieces=(), kind=jnp.bfloat16):
    values = jax.random.normal(stream_key, dims, jnp.float32) * deviation
    if len(pieces) > 0:
        values = levels(stream_key, dims, pieces, -0.22, 0.18) * values
    return jnp.clip(values, min=-bound, max=bound).astype(kind)


def setup_inputs(seed: int = 0, part: int = 0) -> dict:
    key_list = jax.random.split(jax.random.key(seed), 11)
    part_splits = jax.random.split(jax.random.fold_in(key_list[10], part), 11)
    hidden_in = normal_values(part_splits[0], (TOKENS, D), 1.0, 6.0, ((0, 32),))
    queries = draw_queries(jax.random.fold_in(jax.random.fold_in(key_list[10], part), 71), part)
    fresh_kv = draw_fresh_kv(jax.random.fold_in(jax.random.fold_in(key_list[10], part), 71), part)
    stale_kv = draw_stale_kv(jax.random.fold_in(jax.random.fold_in(key_list[10], part), 71), part)
    modulation = normal_values(part_splits[4], (2, D), 0.5, 3.0, (), jnp.float32)
    w_out = normal_values(key_list[5], (HD, D), HD ** -0.5, 0.21875)
    router = normal_values(key_list[6], (D, EXPERTS), D ** -0.5, 0.15625, (), jnp.float32)
    fc_in = normal_values(key_list[7], (2 * EXPERTS, D, FF // 2), D ** -0.5, 0.15625, ((0, 32),))
    fc_out = normal_values(key_list[8], (2 * EXPERTS, FF // 2, D), FF ** -0.5, 0.109375, ((0, 32),))
    expert_ids_keys = jax.random.split(jax.random.fold_in(part_splits[9], 1), TOKENS // TOK_DEV)
    expert_ids_turns = jax.random.permutation(jax.random.fold_in(part_splits[9], 3), TOKENS // TOK_DEV)
    expert_ids = jax.vmap(lambda own, number: assign_block(jax.random.fold_in(part_splits[9], 2), own, number, TOK_DEV, EXPERTS, 2, CAP, 2))(expert_ids_keys, expert_ids_turns).reshape((TOKENS, 2))
    return {"hidden_in": hidden_in, "queries": queries, "fresh_kv": fresh_kv, "stale_kv": stale_kv, "modulation": modulation, "w_out": w_out, "router": router, "fc_in": fc_in, "fc_out": fc_out, "expert_ids": expert_ids}


def attend_block(query_rows, view):
    count = query_rows.shape[0]
    width = HEADS * HEAD
    qh = query_rows.reshape(count, HEADS, HEAD).astype(jnp.float32)
    kh = view[:, :width].reshape(-1, HEADS, HEAD).astype(jnp.float32)
    vh = view[:, width:].reshape(-1, HEADS, HEAD).astype(jnp.float32)
    scores = jnp.einsum('qhd,khd->hqk', qh, kh) * (1.0 / HEAD ** 0.5)
    weights = jax.nn.softmax(scores, axis=-1).astype(jnp.bfloat16)
    out = jnp.einsum('hqk,khd->qhd', weights.astype(jnp.float32), vh)
    return out.reshape(count, width).astype(jnp.bfloat16)

def block_slots(ids):
    onehot = (ids.reshape(-1, 1) == jnp.arange(EXPERTS, dtype=jnp.int32)[None, :]).astype(jnp.int32)
    before = jnp.cumsum(onehot, axis=0) - onehot
    return lax.optimization_barrier(jnp.sum(before * onehot, axis=1)).reshape(ids.shape)

def reference(hidden_in, queries, fresh_kv, stale_kv, modulation, w_out, router, fc_in, fc_out, expert_ids):

    def one_patch(index):
        start = (index * TOK_DEV).astype(jnp.int32)
        rows = lax.dynamic_slice_in_dim(queries, start, TOK_DEV, 0)
        fresh = lax.dynamic_slice_in_dim(fresh_kv, start, TOK_DEV, 0)
        view = lax.dynamic_update_slice_in_dim(stale_kv, fresh, start, 0)
        return attend_block(rows, view)
    attended = lax.map(one_patch, jnp.arange(N_PATCH, dtype=jnp.int32)).reshape(TOKENS, HEADS * HEAD)
    resid = hidden_in.astype(jnp.float32) + jnp.dot(attended, w_out, preferred_element_type=jnp.float32)
    mean = lax.optimization_barrier(jnp.mean(resid, axis=-1, keepdims=True))
    centered = resid - mean
    var = lax.optimization_barrier(jnp.mean(centered * centered, axis=-1, keepdims=True))
    normed = (centered * lax.rsqrt(var + 1e-06) * (1.0 + modulation[0]) + modulation[1]).astype(jnp.bfloat16)
    logits = jnp.dot(normed.astype(jnp.float32), router, precision=lax.Precision.HIGHEST)
    chosen = jnp.take_along_axis(logits, expert_ids, axis=1)
    first_gate = jax.nn.sigmoid(chosen[:, 0] - chosen[:, 1])
    gates = jnp.stack([first_gate, 1.0 - first_gate], axis=1)
    blocks = expert_ids.reshape(N_PATCH, TOK_DEV, 2)
    slots = jax.vmap(block_slots)(blocks)
    position = (blocks * CAP + slots).reshape(N_PATCH, 2 * TOK_DEV)
    copies = jnp.repeat(normed.reshape(N_PATCH, TOK_DEV, D), 2, axis=1)

    def fill(pos, rows):
        return jnp.zeros((EXPERTS * CAP, D), jnp.bfloat16).at[pos].set(rows)
    buffers = jax.vmap(fill)(position, copies).reshape(N_PATCH, EXPERTS, CAP, D)
    per_expert = jnp.transpose(buffers, (1, 0, 2, 3)).reshape(EXPERTS, N_PATCH * CAP, D)
    first = jnp.transpose(fc_in.reshape(EXPERTS, 2, D, FF // 2), (0, 2, 1, 3)).reshape(EXPERTS, D, FF)
    second = fc_out.reshape(EXPERTS, FF, D)

    def run_expert(item):
        rows, w_first, w_second = item
        hidden = jax.nn.gelu(jnp.dot(rows, w_first, preferred_element_type=jnp.float32), approximate=True).astype(jnp.bfloat16)
        return jnp.dot(hidden, w_second, preferred_element_type=jnp.float32)
    outputs = lax.map(run_expert, (per_expert, first, second))
    outputs = jnp.transpose(outputs.reshape(EXPERTS, N_PATCH, CAP, D), (1, 0, 2, 3)).reshape(N_PATCH, EXPERTS * CAP, D)
    picked = jax.vmap(lambda table, pos: jnp.take(table, pos, axis=0))(outputs, position)
    picked = picked.reshape(TOKENS, 2, D)
    moe = lax.optimization_barrier(jnp.sum(gates[:, :, None] * picked, axis=1))
    mixed = (resid + moe).astype(jnp.bfloat16)
    return (attended, mixed)
```

```python
import functools

import jax
import jax.numpy as jnp
from jax import lax
from jax.experimental import pallas as pl
from jax.experimental.pallas import tpu as pltpu
from jax.sharding import Mesh, PartitionSpec as P

NY, NZ = 4, 8
HEADS, HEAD = 8, 96
HD = HEADS * HEAD
TOK = 128
D = 1536
ROW = NZ * TOK
EXPERTS, CAP = 16, 32
F32, BF16 = jnp.float32, jnp.bfloat16
EXP2_SCALE = 1.4426950408889634 / HEAD**0.5
VMEM = pl.BlockSpec(memory_space=pltpu.VMEM)
NT = (((1,), (1,)), ((), ()))


def params(*semantics):
    return pltpu.CompilerParams(
        dimension_semantics=semantics or None, vmem_limit_bytes=48 * 1024 * 1024
    )


def split_heads_kernel(*refs):
    ins, out_ref = refs[:-1], refs[-1]
    at = 0
    for ref in ins:
        turned = ref[...].astype(F32).T.astype(BF16)
        for part in range(turned.shape[0] // HD):
            for h in range(HEADS):
                out_ref[h, at : at + HEAD, :] = turned[part * HD + h * HEAD : part * HD + (h + 1) * HEAD]
            at += HEAD


def split_heads(*arrays):
    rows = sum(a.shape[1] for a in arrays) // HEADS
    return pl.pallas_call(
        split_heads_kernel,
        out_shape=jax.ShapeDtypeStruct((HEADS, rows, TOK), BF16),
        in_specs=[VMEM] * len(arrays),
        out_specs=VMEM,
        compiler_params=params(),
    )(*arrays)


def own_row_kernel(qf_ref, kv_ref, q_ref, m_ref, l_ref, acc_ref, kt, vt):
    i = pl.program_id(0)

    @pl.when(i == 0)
    def _():
        for j in range(NZ):
            kt[:, j * TOK : (j + 1) * TOK] = kv_ref[j, :HEAD]
            vt[:, j * TOK : (j + 1) * TOK] = kv_ref[j, HEAD:]

    cols = pl.ds(pl.multiple_of(i * TOK, TOK), TOK)
    kt[:, cols] = qf_ref[0, HEAD : 2 * HEAD]
    vt[:, cols] = qf_ref[0, 2 * HEAD :]
    q = qf_ref[0, :HEAD].astype(F32).T.astype(BF16)
    s = jnp.dot(q, kt[...], preferred_element_type=F32)
    m = jnp.max(s, axis=1, keepdims=True)
    p = jnp.exp2((s - m) * EXP2_SCALE)
    q_ref[...] = q
    m_ref[...] = m
    l_ref[...] = jnp.sum(p, axis=1, keepdims=True)
    acc_ref[...] = lax.dot_general(p.astype(BF16), vt[...], NT, preferred_element_type=F32)
    kt[:, cols] = kv_ref[i, :HEAD]
    vt[:, cols] = kv_ref[i, HEAD:]


def attend_own_row(qf, kv):
    row = lambda width: pl.BlockSpec((TOK, width), lambda i: (i, 0))
    return pl.pallas_call(
        own_row_kernel,
        grid=(NZ,),
        out_shape=(
            jax.ShapeDtypeStruct((ROW, HEAD), BF16),
            jax.ShapeDtypeStruct((ROW, 1), F32),
            jax.ShapeDtypeStruct((ROW, 1), F32),
            jax.ShapeDtypeStruct((ROW, HEAD), F32),
        ),
        in_specs=[
            pl.BlockSpec((1, 3 * HEAD, TOK), lambda i: (i, 0, 0)),
            pl.BlockSpec((NZ, 2 * HEAD, TOK), lambda i: (0, 0, 0)),
        ],
        out_specs=(row(HEAD), row(1), row(1), row(HEAD)),
        scratch_shapes=[pltpu.VMEM((HEAD, ROW), BF16), pltpu.VMEM((HEAD, ROW), BF16)],
        compiler_params=params("arbitrary"),
        cost_estimate=pl.CostEstimate(
            flops=4 * ROW * ROW * HEAD, bytes_accessed=4 << 20, transcendentals=ROW * ROW
        ),
    )(qf, kv)


def other_rows_kernel(last, tile, n, *refs):
    kv_refs = refs[:n]
    q_ref, m_in, l_in, acc_in = refs[n : n + 4]
    outs, (kt, vt) = refs[n + 4 : -2], refs[-2:]

    @pl.when(pl.program_id(0) == 0)
    def _():
        for c, ref in enumerate(kv_refs):
            for j in range(ref.shape[0]):
                at = c * ROW + j * TOK
                kt[:, at : at + TOK] = ref[j, :HEAD]
                vt[:, at : at + TOK] = ref[j, HEAD:]

    q = q_ref[...]
    m, l, acc = m_in[...], l_in[...], acc_in[...]
    for c in range(n):
        cols = slice(c * ROW, (c + 1) * ROW)
        s = jnp.dot(q, kt[:, cols], preferred_element_type=F32)
        top = jnp.maximum(m, jnp.max(s, axis=1, keepdims=True))
        p = jnp.exp2((s - top) * EXP2_SCALE)
        fade = jnp.exp2((m - top) * EXP2_SCALE)
        l = l * fade + jnp.sum(p, axis=1, keepdims=True)
        acc = acc * fade + lax.dot_general(
            p.astype(BF16), vt[:, cols], NT, preferred_element_type=F32
        )
        m = top
    if last:
        outs[0][...] = (acc / l).T.astype(BF16)
    else:
        outs[0][...] = m
        outs[1][...] = l
        outs[2][...] = acc


def attend_other_rows(kvs, state, last, tile=512):
    q, m, l, acc = state
    n = len(kvs)
    row = lambda width: pl.BlockSpec((tile, width), lambda i: (i, 0))
    if last:
        out_shape = (jax.ShapeDtypeStruct((HEAD, ROW), BF16),)
        out_specs = (pl.BlockSpec((HEAD, tile), lambda i: (0, i)),)
    else:
        out_shape = tuple(jax.ShapeDtypeStruct((ROW, w), F32) for w in (1, 1, HEAD))
        out_specs = (row(1), row(1), row(HEAD))
    return pl.pallas_call(
        functools.partial(other_rows_kernel, last, tile, n),
        grid=(ROW // tile,),
        out_shape=out_shape,
        in_specs=[pl.BlockSpec(a.shape, lambda i: (0, 0, 0)) for a in kvs]
        + [row(HEAD), row(1), row(1), row(HEAD)],
        out_specs=out_specs,
        scratch_shapes=[pltpu.VMEM((HEAD, n * ROW), BF16), pltpu.VMEM((HEAD, n * ROW), BF16)],
        compiler_params=params("arbitrary"),
        cost_estimate=pl.CostEstimate(
            flops=4 * ROW * n * ROW * HEAD, bytes_accessed=5 << 20, transcendentals=n * ROW * ROW
        ),
    )(*kvs, q, m, l, acc)


def norm_kernel(pos, hid_ref, att_ref, wo_ref, mod_ref, rt_ref, ids_ref, x_ref, g_ref, res_ref, out_ref):
    r = pl.program_id(0)
    y, z = pos[0], pos[1]
    block = lax.rem(z + r, NZ)
    cols = pl.ds(pl.multiple_of(block * TOK, TOK), TOK)
    att = att_ref[:, cols].astype(F32).T.astype(BF16)
    resid = hid_ref[0].astype(F32) + jnp.dot(att, wo_ref[...], preferred_element_type=F32)
    centered = resid - jnp.mean(resid, axis=1, keepdims=True)
    var = jnp.mean(centered * centered, axis=1, keepdims=True)
    normed = (centered * lax.rsqrt(var + 1e-06) * (1.0 + mod_ref[0:1]) + mod_ref[1:2]).astype(BF16)

    @pl.when(r == 0)
    def _():
        res_ref[...] = resid
        out_ref[...] = att

    logits = jnp.dot(normed, rt_ref[...], preferred_element_type=F32)
    logits = logits[:, 256:384] + logits[:, 128:256] + logits[:, :128]
    id0, id1 = ids_ref[0, :, 0:1], ids_ref[0, :, 1:2]
    lane = lax.broadcasted_iota(jnp.int32, (TOK, TOK), 1)
    token = lax.broadcasted_iota(jnp.int32, (TOK, TOK), 0)
    zero = jnp.zeros((TOK, TOK), F32)
    c0 = jnp.sum(jnp.where(lane == id0, logits, zero), axis=1, keepdims=True)
    c1 = jnp.sum(jnp.where(lane == id1, logits, zero), axis=1, keepdims=True)
    gate0 = jax.nn.sigmoid(c0 - c1)
    gate1 = 1.0 - gate0
    expert = ((y + lane // CAP) % NY) * NY + z // 2
    first, second = expert == id0, expert == id1
    chosen = jnp.where(first | second, 1.0, 0.0)
    earlier = jnp.where(lane < token, 1.0, 0.0).astype(BF16)
    before = jnp.dot(earlier, chosen.astype(BF16), preferred_element_type=F32)
    hit = jnp.where(before == (lane % CAP).astype(F32), chosen, zero)
    gate = hit * jnp.where(first, gate0, gate1)
    high = gate.astype(BF16)
    g_ref[0, :, :TOK] = high
    g_ref[0, :, TOK:] = (gate - high.astype(F32)).astype(BF16)
    rows = jnp.dot(hit.T.astype(BF16), normed, preferred_element_type=F32).astype(BF16)
    for e in range(NY):
        x_ref[e, 0] = rows[e * CAP : (e + 1) * CAP]


def norm_and_dispatch(pos, hid, att, w_out, modulation, router3, ids):
    whole = lambda a: pl.BlockSpec(a.shape, lambda r, pos: (0,) * a.ndim)
    turn = lambda r, pos: (lax.rem(pos[1] + r, NZ), 0, 0)
    return pl.pallas_call(
        norm_kernel,
        grid_spec=pltpu.PrefetchScalarGridSpec(
            num_scalar_prefetch=1,
            grid=(NZ,),
            in_specs=[
                pl.BlockSpec((1, TOK, D), turn),
                whole(att),
                whole(w_out),
                whole(modulation),
                whole(router3),
                pl.BlockSpec((1, TOK, 2), turn),
            ],
            out_specs=(
                pl.BlockSpec((NY, 1, CAP, D), lambda r, pos: (0, r, 0, 0)),
                pl.BlockSpec((1, TOK, 2 * TOK), lambda r, pos: (r, 0, 0)),
                pl.BlockSpec((TOK, D), lambda r, pos: (0, 0)),
                pl.BlockSpec((TOK, HD), lambda r, pos: (0, 0)),
            ),
        ),
        out_shape=(
            jax.ShapeDtypeStruct((NY, NZ, CAP, D), BF16),
            jax.ShapeDtypeStruct((NZ, TOK, 2 * TOK), BF16),
            jax.ShapeDtypeStruct((TOK, D), F32),
            jax.ShapeDtypeStruct((TOK, HD), BF16),
        ),
        compiler_params=params("arbitrary"),
        cost_estimate=pl.CostEstimate(
            flops=2 * ROW * D * (HD + 512), bytes_accessed=16 << 20, transcendentals=ROW
        ),
    )(pos, hid, att, w_out, modulation, router3, ids)


def expert_kernel(x_ref, w1_ref, w2_ref, o_ref, acc):
    j = pl.program_id(0)
    hidden = jax.nn.gelu(
        jnp.dot(x_ref[...], w1_ref[...], preferred_element_type=F32), approximate=True
    ).astype(BF16)
    term = jnp.dot(hidden, w2_ref[...], preferred_element_type=F32)

    @pl.when(j == 0)
    def _():
        acc[...] = term

    @pl.when(j > 0)
    def _():
        acc[...] += term

    @pl.when(j == pl.num_programs(0) - 1)
    def _():
        o_ref[...] = acc[...].astype(BF16)


def expert(x, w1, w2, tile=512):
    n = x.shape[0]
    return pl.pallas_call(
        expert_kernel,
        grid=(D // tile,),
        out_shape=jax.ShapeDtypeStruct((n, D), BF16),
        in_specs=[
            pl.BlockSpec((n, D), lambda j: (0, 0)),
            pl.BlockSpec((D, tile), lambda j: (0, j)),
            pl.BlockSpec((tile, D), lambda j: (j, 0)),
        ],
        out_specs=pl.BlockSpec((n, D), lambda j: (0, 0)),
        scratch_shapes=[pltpu.VMEM((n, D), F32)],
        compiler_params=params("arbitrary"),
        cost_estimate=pl.CostEstimate(
            flops=4 * n * D * D, bytes_accessed=11 << 20, transcendentals=n * D
        ),
    )(x, w1, w2)


def combine_kernel(g_ref, y0, y1, y2, y3, res_ref, part_ref, own_ref):
    r = pl.program_id(0)
    rows = jnp.concatenate([y0[0], y1[0], y2[0], y3[0]], axis=0)
    rows = jnp.concatenate([rows, rows], axis=0)
    total = jnp.dot(g_ref[0], rows, preferred_element_type=F32)
    part_ref[0] = total.astype(BF16)

    @pl.when(r == 0)
    def _():
        own_ref[...] = res_ref[...] + total


def combine(gates, ys, resid):
    block = pl.BlockSpec((1, CAP, D), lambda r: (r, 0, 0))
    own = pl.BlockSpec((TOK, D), lambda r: (0, 0))
    return pl.pallas_call(
        combine_kernel,
        grid=(NZ,),
        out_shape=(
            jax.ShapeDtypeStruct((NZ, TOK, D), BF16),
            jax.ShapeDtypeStruct((TOK, D), F32),
        ),
        in_specs=[pl.BlockSpec((1, TOK, 2 * TOK), lambda r: (r, 0, 0))] + [block] * 4 + [own],
        out_specs=(pl.BlockSpec((1, TOK, D), lambda r: (r, 0, 0)), own),
        compiler_params=params("arbitrary"),
        cost_estimate=pl.CostEstimate(
            flops=4 * ROW * TOK * D, bytes_accessed=8 << 20, transcendentals=0
        ),
    )(gates, *ys, resid)


def send(x, axis, n, shift):
    return lax.ppermute(x, axis, [(i, (i + shift) % n) for i in range(n)])


def after(x, *done):
    return lax.optimization_barrier((x,) + done)[0]


def gather_z(x):
    return lax.all_gather(x, "z", axis=0, tiled=False)


def gather_rows_z(x):
    z = lax.axis_index("z")
    out = jnp.zeros((NZ,) + x.shape, x.dtype)
    place = lambda out, block, at: lax.dynamic_update_slice(out, block[None], (at % NZ, 0, 0))
    out = place(out, x, z)
    up, down = x, x
    for s in range(1, 4):
        up, down = send(up, "z", NZ, 1), send(down, "z", NZ, -1)
        out = place(out, up, z + NZ - s)
        out = place(out, down, z + s)
    half = x.shape[0] // 2
    up, down = send(up[:half], "z", NZ, 1), send(down[half:], "z", NZ, -1)
    return place(out, jnp.concatenate([up, down], axis=0), z + 4)


def scatter_sum_z(parts, own):
    half = TOK // 2
    down, up = send(parts[4][:half], "z", NZ, -1), send(parts[4][half:], "z", NZ, 1)
    add = lambda a, b: (a.astype(F32) + b.astype(F32)).astype(BF16)
    down = jnp.concatenate([add(parts[5][:half], down), parts[5][half:]], axis=0)
    up = jnp.concatenate([parts[3][:half], add(parts[3][half:], up)], axis=0)
    for s in (6, 7):
        down, up = send(down, "z", NZ, -1), send(up, "z", NZ, 1)
        down, up = add(parts[s], down), add(parts[NZ - s], up)
    down, up = send(down, "z", NZ, -1), send(up, "z", NZ, 1)
    return (own + down.astype(F32) + up.astype(F32)).astype(BF16)


def per_device(
    hidden_in, queries, fresh_kv, stale_kv, modulation, w_out, router, fc_in, fc_out, expert_ids
):
    y, z = lax.axis_index("y"), lax.axis_index("z")
    pos = jnp.stack([y, z]).astype(jnp.int32)
    batch = lax.axis_size("batch")

    def neighbour(w):
        rows = D // batch
        part = lax.dynamic_slice_in_dim(w, lax.axis_index("batch") * rows, rows, 0)
        return lax.all_gather(send(part, "y", NY, -1), "batch", axis=0, tiled=True)

    w1, w2 = fc_in[0], fc_out[0]
    w1_next, w2_next = neighbour(w1), neighbour(w2)

    kv = lax.all_to_all(split_heads(stale_kv), "z", split_axis=0, concat_axis=0, tiled=True)
    qf = lax.all_to_all(
        split_heads(after(queries, kv), fresh_kv), "z", split_axis=0, concat_axis=0, tiled=True
    )
    ids = gather_z(after(expert_ids, kv))
    hid = gather_z(after(hidden_in, kv))
    kv_prev, kv_next = send(kv, "y", NY, 1), send(kv, "y", NY, -1)
    kv_far = [send(kv_prev[:4], "y", NY, 1), send(kv_next[4:], "y", NY, -1)]
    q, m, l, acc = attend_own_row(qf, kv)
    m, l, acc = attend_other_rows([kv_prev, kv_next], (q, m, l, acc), False)
    (att,) = attend_other_rows([jnp.concatenate(kv_far, axis=0)], (q, m, l, acc), True)
    att = gather_rows_z(att).reshape(HD, ROW)

    pieces, rest = [], router
    for _ in range(3):
        piece = lax.reduce_precision(rest, exponent_bits=8, mantissa_bits=7)
        rest = rest - piece
        pieces.append(jnp.pad(piece.astype(BF16), ((0, 0), (0, TOK - EXPERTS))))
    router3 = jnp.concatenate(pieces, axis=1)
    x, gates, resid, attended = norm_and_dispatch(
        pos, hid, att, w_out, modulation, router3, ids
    )
    x = [x[e].reshape(NZ * CAP, D) for e in range(NY)]

    x_prev, x_next = send(x[2], "y", NY, 1), send(x[3], "y", NY, -1)
    y0 = expert(x[0], w1, w2)
    y3 = send(expert(x_next, w1, w2), "y", NY, 1)
    y1 = expert(x[1], w1_next, w2_next)
    y2 = send(expert(x_prev, w1_next, w2_next), "y", NY, -1)
    ys = [a.reshape(NZ, CAP, D) for a in (y0, y1, y2, y3)]
    parts, own = combine(gates, ys, resid)
    return attended, scatter_sum_z(parts, own)


def solution(mesh):
    split = Mesh(mesh.devices.reshape(NY, NZ, -1), ("y", "z", "batch"))
    tokens = P(("batch", "y", "z"), None)
    return jax.shard_map(
        per_device,
        mesh=split,
        in_specs=(
            tokens,
            tokens,
            tokens,
            tokens,
            P("batch", None),
            P(),
            P(),
            P(("y", "z"), None, None),
            P(("y", "z"), None, None),
            tokens,
        ),
        out_specs=(tokens, tokens),
        check_vma=False,
    )
```

```python
import functools

import jax
import jax.numpy as jnp
from jax import lax
from jax.experimental import pallas as pl
from jax.experimental.pallas import tpu as pltpu
from jax.sharding import Mesh, PartitionSpec as P

NY, NZ = 4, 8
GROUP = 4
FAR, NEAR = (2, 3, 4, 5), (6, 7, 0, 1)
CHUNK = 128
HEADS, HEAD = 8, 96
HD = HEADS * HEAD
TOK = 128
D = 1536
ROW = NZ * TOK
EXPERTS, CAP = 16, 32
SLICE = 192
IDS = 16
F32, BF16 = jnp.float32, jnp.bfloat16
EXP2_SCALE = 1.4426950408889634 / HEAD**0.5
VMEM = pl.BlockSpec(memory_space=pltpu.VMEM)
NT = (((1,), (1,)), ((), ()))


def params(*semantics):
    return pltpu.CompilerParams(
        dimension_semantics=semantics or None, vmem_limit_bytes=28 * 1024 * 1024
    )


def split_heads_kernel(*refs):
    ins, out_ref = refs[:-1], refs[-1]
    at = 0
    for ref in ins:
        turned = ref[...].astype(F32).T.astype(BF16)
        if turned.shape[0] < HD:
            for h in range(HEADS):
                out_ref[h, at : at + turned.shape[0], :] = turned
            at += turned.shape[0]
        for part in range(turned.shape[0] // HD):
            for h in range(HEADS):
                out_ref[h, at : at + HEAD, :] = turned[part * HD + h * HEAD : part * HD + (h + 1) * HEAD]
            at += HEAD


def split_heads(*arrays):
    rows = sum(a.shape[1] // HEADS if a.shape[1] >= HD else a.shape[1] for a in arrays)
    return pl.pallas_call(
        split_heads_kernel,
        out_shape=jax.ShapeDtypeStruct((HEADS, rows, TOK), BF16),
        in_specs=[VMEM] * len(arrays),
        out_specs=VMEM,
        compiler_params=params(),
    )(*arrays)


def update(q, kt, vt, state):
    s = jnp.dot(q, kt, preferred_element_type=F32)
    top = jnp.max(s, axis=1, keepdims=True)
    if state is not None:
        m, l, acc = state
        top = jnp.maximum(m, top)
    p = jnp.exp2((s - top) * EXP2_SCALE)
    total = jnp.sum(p, axis=1, keepdims=True)
    out = lax.dot_general(p.astype(BF16), vt, NT, preferred_element_type=F32)
    if state is not None:
        fade = jnp.exp2((m - top) * EXP2_SCALE)
        total, out = total + l * fade, out + acc * fade
    return top, total, out


def fill(refs, kt, vt):
    @pl.when(pl.program_id(0) == 0)
    def _():
        at = 0
        for ref in refs:
            for j in range(ref.shape[0]):
                kt[:, at : at + TOK] = ref[j, :HEAD]
                vt[:, at : at + TOK] = ref[j, HEAD : 2 * HEAD]
                at += TOK


def own_row_kernel(own_ref, all_ref, q_ref, m_ref, l_ref, acc_ref, kt, vt):
    i = pl.program_id(0)
    fill((all_ref,), kt, vt)
    cols = pl.ds(pl.multiple_of(i * TOK, TOK), TOK)
    kt[:, cols] = own_ref[0, 3 * HEAD : 4 * HEAD]
    vt[:, cols] = own_ref[0, 4 * HEAD : 5 * HEAD]
    q = own_ref[0, 2 * HEAD : 3 * HEAD].astype(F32).T.astype(BF16)
    q_ref[...] = q
    m_ref[...], l_ref[...], acc_ref[...] = update(q, kt[...], vt[...], None)
    kt[:, cols] = all_ref[i, :HEAD]
    vt[:, cols] = all_ref[i, HEAD : 2 * HEAD]


WIDTHS = ((HEAD, BF16), (1, F32), (1, F32), (HEAD, F32))


def attend_own_row(rows):
    return pl.pallas_call(
        own_row_kernel,
        grid=(NZ,),
        out_shape=tuple(jax.ShapeDtypeStruct((ROW, w), t) for w, t in WIDTHS),
        in_specs=[
            pl.BlockSpec((1,) + rows.shape[1:], lambda i: (i, 0, 0)),
            pl.BlockSpec((NZ, 2 * HEAD, TOK), lambda i: (0, 0, 0)),
        ],
        out_specs=tuple(pl.BlockSpec((TOK, w), lambda i: (i, 0)) for w, _ in WIDTHS),
        scratch_shapes=[pltpu.VMEM((HEAD, ROW), BF16), pltpu.VMEM((HEAD, ROW), BF16)],
        compiler_params=params("arbitrary"),
        cost_estimate=pl.CostEstimate(
            flops=4 * ROW * ROW * HEAD, bytes_accessed=4 << 20, transcendentals=ROW * ROW
        ),
    )(rows, rows)


def other_rows_kernel(last, n, kvs, *refs):
    kv_refs, (q_ref, m_in, l_in, acc_in), outs = refs[:kvs], refs[kvs : kvs + 4], refs[kvs + 4 : -2]
    kt, vt = refs[-2:]
    fill(kv_refs, kt, vt)
    state = m_in[...], l_in[...], acc_in[...]
    for c in range(n):
        cols = slice(c * ROW, (c + 1) * ROW)
        state = update(q_ref[...], kt[:, cols], vt[:, cols], state)
    if last:
        outs[0][...] = (state[2] / state[1]).T.astype(BF16)
    else:
        outs[0][...], outs[1][...], outs[2][...] = state


def attend_other_rows(kvs, state, last, tile=512):
    n = sum(a.shape[0] for a in kvs) // NZ
    row = lambda width: pl.BlockSpec((tile, width), lambda i: (i, 0))
    if last:
        out_shape = jax.ShapeDtypeStruct((HEAD, ROW), BF16)
        out_specs = pl.BlockSpec((HEAD, tile), lambda i: (0, i))
    else:
        out_shape = tuple(jax.ShapeDtypeStruct((ROW, w), t) for w, t in WIDTHS[1:])
        out_specs = tuple(row(w) for w, _ in WIDTHS[1:])
    return pl.pallas_call(
        functools.partial(other_rows_kernel, last, n, len(kvs)),
        grid=(ROW // tile,),
        out_shape=out_shape,
        in_specs=[pl.BlockSpec(a.shape, lambda i: (0, 0, 0)) for a in kvs]
        + [row(w) for w, _ in WIDTHS],
        out_specs=out_specs,
        scratch_shapes=[pltpu.VMEM((HEAD, n * ROW), BF16), pltpu.VMEM((HEAD, n * ROW), BF16)],
        compiler_params=params("arbitrary"),
        cost_estimate=pl.CostEstimate(
            flops=4 * ROW * n * ROW * HEAD, bytes_accessed=5 << 20, transcendentals=n * ROW * ROW
        ),
    )(*kvs, *state)


def norm_kernel(own, pos, *refs):
    hid_refs, ids_refs, att_refs = refs[:GROUP], refs[GROUP : 2 * GROUP], refs[2 * GROUP : 3 * GROUP]
    wo_ref, mod_ref, rt_ref = refs[3 * GROUP : 3 * GROUP + 3]
    x_refs, g_ref, normed_ref = refs[3 * GROUP + 3 : 3 * GROUP + 3 + NY], refs[3 * GROUP + 3 + NY], refs[-1]
    if own is not None:
        res_ref, out_ref = refs[-3:-1]
    y, z = pos[0], pos[1]
    many = GROUP * TOK
    att = jnp.concatenate([ref[...] for ref in att_refs], axis=1).astype(F32).T.astype(BF16)
    scale, shift = 1.0 + mod_ref[0:1], mod_ref[1:2]
    for i in range(GROUP):
        for j in range(0, TOK, CHUNK):
            at = slice(i * TOK + j, i * TOK + j + CHUNK)
            resid = jnp.dot(att[at], wo_ref[...], preferred_element_type=F32)
            resid = resid + hid_refs[i][0, j : j + CHUNK].astype(F32)
            centered = resid - jnp.mean(resid, axis=1, keepdims=True)
            var = jnp.mean(centered * centered, axis=1, keepdims=True)
            normed_ref[at] = (centered * lax.rsqrt(var + 1e-06) * scale + shift).astype(BF16)
            if i == own:
                res_ref[j : j + CHUNK] = resid

    if own is not None:
        out_ref[...] = att[own * TOK : (own + 1) * TOK]

    normed = normed_ref[...]
    logits = jnp.dot(normed, rt_ref[...], preferred_element_type=F32)
    ids = jnp.concatenate([ref[0] for ref in ids_refs], axis=1).astype(F32).T.astype(jnp.int32)
    id0, id1 = ids[:, 0:1], ids[:, 1:2]
    lane = lax.broadcasted_iota(jnp.int32, (many, TOK), 1)
    zero = jnp.zeros((many, TOK), F32)
    logits = jnp.where(lane < 3 * EXPERTS, logits, zero)
    c0 = jnp.sum(jnp.where(lane % EXPERTS == id0, logits, zero), axis=1, keepdims=True)
    c1 = jnp.sum(jnp.where(lane % EXPERTS == id1, logits, zero), axis=1, keepdims=True)
    gate0 = jax.nn.sigmoid(c0 - c1)
    gate1 = 1.0 - gate0
    expert = ((y + lane // CAP) % NY) * NY + z // 2
    first, second = expert == id0, expert == id1
    chosen = jnp.where(first | second, 1.0, 0.0)
    gate = jnp.where(first, gate0, gate1)
    slot = (lane[:TOK] % CAP).astype(F32)
    token = lax.broadcasted_iota(jnp.int32, (TOK, TOK), 0)
    earlier = jnp.where(lane[:TOK] < token, 1.0, 0.0).astype(BF16)
    for i in range(GROUP):
        at = slice(i * TOK, (i + 1) * TOK)
        before = jnp.dot(earlier, chosen[at].astype(BF16), preferred_element_type=F32)
        hit = jnp.where(before == slot, chosen[at], 0.0)
        weight = hit * gate[at]
        high = weight.astype(BF16)
        g_ref[i, :, :TOK] = high
        g_ref[i, :, TOK:] = (weight - high.astype(F32)).astype(BF16)
        rows = jnp.dot(hit.T.astype(BF16), normed[at], preferred_element_type=F32).astype(BF16)
        for e in range(NY):
            x_refs[e][i] = rows[e * CAP : (e + 1) * CAP]


def norm_and_dispatch(blocks, pos, hid, att, w_out, modulation, router3, rows):
    n = len(blocks)
    own = 0 in blocks
    whole = lambda a: pl.BlockSpec(a.shape, lambda r, pos: (0,) * a.ndim)
    block = lambda i, r, pos: lax.rem(pos[1] + blocks[0] + r * GROUP + i, NZ)
    hids = [
        pl.BlockSpec((1, TOK, D), lambda r, pos, i=i: (block(i, r, pos), 0, 0)) for i in range(GROUP)
    ]
    ids = [
        pl.BlockSpec((1, IDS, TOK), lambda r, pos, i=i: (block(i, r, pos), 5 * HEAD // IDS, 0))
        for i in range(GROUP)
    ]
    atts = [pl.BlockSpec((HD, TOK), lambda r, pos, i=i: (0, block(i, r, pos))) for i in range(GROUP)]
    outs = [((n, CAP, D), BF16, (GROUP, CAP, D))] * NY + [((n, TOK, 2 * TOK), BF16, (GROUP, TOK, 2 * TOK))]
    if own:
        outs += [((TOK, D), F32, None), ((TOK, HD), BF16, None)]
    return pl.pallas_call(
        functools.partial(norm_kernel, blocks.index(0) if own else None),
        grid_spec=pltpu.PrefetchScalarGridSpec(
            num_scalar_prefetch=1,
            grid=(n // GROUP,),
            in_specs=hids + ids + atts + [whole(w_out), whole(modulation), whole(router3)],
            out_specs=tuple(
                pl.BlockSpec(tile, lambda r, pos: (r, 0, 0))
                if tile
                else pl.BlockSpec(shape, lambda r, pos: (0, 0))
                for shape, _, tile in outs
            ),
            scratch_shapes=[pltpu.VMEM((GROUP * TOK, D), BF16)],
        ),
        out_shape=tuple(jax.ShapeDtypeStruct(shape, t) for shape, t, _ in outs),
        compiler_params=params("arbitrary"),
        cost_estimate=pl.CostEstimate(
            flops=2 * n * TOK * D * (HD + 256), bytes_accessed=8 << 20, transcendentals=ROW
        ),
    )(pos, *[hid] * GROUP, *[rows] * GROUP, *[att] * GROUP, w_out, modulation, router3)


def expert_kernel(pick, tile, xa_ref, xb_ref, *refs):
    w_refs, (oa_ref, ob_ref, w1, w2, hidden, sems) = refs[:-6], refs[-6:]
    n = xa_ref.shape[0]
    steps = D // tile
    copies = []
    for p, held in enumerate((w1, w2)):
        for c in range(steps):
            cols = pl.ds(c * tile, tile)
            source = w_refs[0].at[:, p, :, cols] if pick else w_refs[p].at[:, :, cols]
            copy = pltpu.make_async_copy(source, held.at[:, :, cols], sems.at[p * steps + c])
            copy.start()
            copies.append(copy)
    x = jnp.concatenate([xa_ref[...], xb_ref[...]], axis=0)
    for c in range(steps):
        cols = slice(c * tile, (c + 1) * tile)
        copies[c].wait()
        first = jnp.dot(x, w1[:, :, cols].reshape(D, tile), preferred_element_type=F32)
        hidden[:, cols] = jax.nn.gelu(first, approximate=True).astype(BF16)
    for c in range(steps):
        cols = slice(c * tile, (c + 1) * tile)
        copies[steps + c].wait()
        out = jnp.dot(hidden[...], w2[:, :, cols].reshape(D, tile), preferred_element_type=F32)
        oa_ref[:, cols] = out[:n].astype(BF16)
        ob_ref[:, cols] = out[n:].astype(BF16)


def expert(xa, xb, *weights, tile=512):
    shape = xa.shape
    xa, xb = xa.reshape(-1, D), xb.reshape(-1, D)
    n = xa.shape[0]
    held = (D // SLICE, SLICE, D)
    pick = len(weights) == 1
    if not pick:
        weights = [w.reshape(held) for w in weights]
    ya, yb = pl.pallas_call(
        functools.partial(expert_kernel, pick, tile),
        out_shape=(jax.ShapeDtypeStruct((n, D), BF16),) * 2,
        in_specs=[VMEM, VMEM] + [pl.BlockSpec(memory_space=pl.ANY)] * len(weights),
        out_specs=(VMEM, VMEM),
        scratch_shapes=[
            pltpu.VMEM(held, BF16),
            pltpu.VMEM(held, BF16),
            pltpu.VMEM((2 * n, D), BF16),
            pltpu.SemaphoreType.DMA((2 * D // tile,)),
        ],
        compiler_params=params(),
        cost_estimate=pl.CostEstimate(
            flops=8 * n * D * D, bytes_accessed=11 << 20, transcendentals=2 * n * D
        ),
    )(xa, xb, *weights)
    return ya.reshape(shape), yb.reshape(shape)


def combine_kernel(blocks, *refs):
    g_ref, ys, outs = refs[0], refs[1:5], refs[5:]
    if 0 in blocks:
        res_ref, outs = outs[0], outs[1:]
    for i, (block, out) in enumerate(zip(blocks, outs)):
        rows = jnp.concatenate([y[i] for y in ys], axis=0)
        total = jnp.dot(g_ref[i, :, :TOK], rows, preferred_element_type=F32)
        total = total + jnp.dot(g_ref[i, :, TOK:], rows, preferred_element_type=F32)
        if block == 0:
            total = total + res_ref[...]
        out[...] = total.astype(out.dtype)


def combine(blocks, gates, ys, *resid):
    return pl.pallas_call(
        functools.partial(combine_kernel, blocks),
        out_shape=tuple(
            jax.ShapeDtypeStruct((TOK, D), F32 if i == 0 else BF16) for i in blocks
        ),
        in_specs=[VMEM] * (5 + len(resid)),
        out_specs=(VMEM,) * len(blocks),
        compiler_params=params(),
        cost_estimate=pl.CostEstimate(
            flops=4 * len(blocks) * TOK * TOK * D, bytes_accessed=4 << 20, transcendentals=0
        ),
    )(gates, *ys, *resid)


def send(x, axis, n, shift):
    return lax.ppermute(x, axis, [(i, (i + shift) % n) for i in range(n)])


def after(x, *done):
    return lax.optimization_barrier((x,) + done)[0]


def ring_z(x):
    got = [x] + [None] * (NZ - 1)
    up, down = x, x
    for s in range(1, 4):
        up, down = send(up, "z", NZ, 1), send(down, "z", NZ, -1)
        got[NZ - s], got[s] = up, down
    half = x.shape[0] // 2
    up, down = send(up[:half], "z", NZ, 1), send(down[half:], "z", NZ, -1)
    got[4] = jnp.concatenate([up, down], axis=0)
    return got


def in_order(blocks):
    z = lax.axis_index("z")
    out = jnp.zeros((NZ,) + blocks[0].shape, blocks[0].dtype)
    for r, block in enumerate(blocks):
        out = lax.dynamic_update_slice(out, block[None], ((z + r) % NZ, 0, 0))
    return out


def add(a, b):
    return (a.astype(F32) + b.astype(F32)).astype(BF16)


def scatter_first(parts):
    half = TOK // 2
    down, up = send(parts[4][:half], "z", NZ, -1), send(parts[4][half:], "z", NZ, 1)
    down = jnp.concatenate([add(parts[5][:half], down), parts[5][half:]], axis=0)
    up = jnp.concatenate([parts[3][:half], add(parts[3][half:], up)], axis=0)
    return lax.optimization_barrier((down, up))


def scatter_rest(parts, down, up):
    for s in (6, 7):
        down, up = send(down, "z", NZ, -1), send(up, "z", NZ, 1)
        down, up = add(parts[s], down), add(parts[NZ - s], up)
        down, up = lax.optimization_barrier((down, up))
    down, up = send(down, "z", NZ, -1), send(up, "z", NZ, 1)
    return (parts[0] + down.astype(F32) + up.astype(F32)).astype(BF16)


def per_device(
    hidden_in, queries, fresh_kv, stale_kv, modulation, w_out, router, fc_in, fc_out, expert_ids
):
    y, z = lax.axis_index("y"), lax.axis_index("z")
    pos = jnp.stack([y, z]).astype(jnp.int32)
    batch = lax.axis_size("batch")

    rows = D // batch
    w1, w2 = fc_in[0], fc_out[0]
    at = lax.axis_index("batch") * rows
    part = jnp.concatenate(
        [lax.dynamic_slice_in_dim(w, at, rows, 0) for w in (w1, w2)], axis=0
    )
    ids = jnp.pad(expert_ids.astype(BF16), ((0, 0), (0, IDS - 2)))
    heads = split_heads(after(stale_kv, part), queries, fresh_kv, ids)
    row = lax.all_to_all(heads, "z", split_axis=0, concat_axis=0, tiled=True)
    row, part_next = lax.optimization_barrier((row, send(part, "y", NY, -1)))
    hid = lax.all_gather(hidden_in, "z", axis=0, tiled=False)
    kv = row[:, : 2 * HEAD]
    kv_prev, kv_next = send(kv, "y", NY, 1), send(kv, "y", NY, -1)
    state = attend_own_row(row)
    kv_prev, kv_next, *state = lax.optimization_barrier((kv_prev, kv_next, *state))
    kv_far = [send(kv_prev[:4], "y", NY, 1), send(kv_next[4:], "y", NY, -1)]
    w_next = lax.all_gather(after(part_next, *state), "batch", axis=0, tiled=False)
    w_next = w_next.reshape(batch, 2, rows, D)
    state = (state[0], *attend_other_rows([kv_prev, kv_next], state, False))
    att = attend_other_rows(kv_far, state, True)
    att = in_order(ring_z(att)).reshape(HD, ROW)

    pieces, rest = [], router
    for _ in range(3):
        piece = lax.reduce_precision(rest, exponent_bits=8, mantissa_bits=7)
        rest = rest - piece
        pieces.append(piece.astype(BF16))
    router3 = jnp.pad(jnp.concatenate(pieces, axis=1), ((0, 0), (0, TOK - 3 * EXPERTS)))
    groups = []
    for blocks in (FAR, NEAR):
        x0, x1, x2, x3, gates, *own = norm_and_dispatch(
            blocks, pos, hid, att, w_out, modulation, router3, row
        )
        att = after(att, x2)
        groups.append((blocks, x0, x1, send(x2, "y", NY, 1), send(x3, "y", NY, -1), gates, own))
    attended = own[1]

    ys, last = [], ()
    for _, x0, x1, x_prev, x_next, _, _ in groups:
        y0, y3 = expert(after(x0, *last), x_next, w1, w2)
        y1, y2 = expert(after(x1, y0), x_prev, w_next)
        ys.append((y0, y1, send(y2, "y", NY, -1), send(y3, "y", NY, 1)))
        last = (y1,)
    (_, *_, far_gates, _), (_, *_, near_gates, own) = groups
    parts = dict(zip(FAR, combine(FAR, after(far_gates, *last), ys[0])))
    sums = scatter_first(parts)
    parts |= dict(zip(NEAR, combine(NEAR, after(near_gates, *sums), ys[1], own[0])))
    return attended, scatter_rest(parts, *sums)


def solution(mesh):
    split = Mesh(mesh.devices.reshape(NY, NZ, -1), ("y", "z", "batch"))
    tokens = P(("batch", "y", "z"), None)
    return jax.shard_map(
        per_device,
        mesh=split,
        in_specs=(
            tokens,
            tokens,
            tokens,
            tokens,
            P("batch", None),
            P(),
            P(),
            P(("y", "z"), None, None),
            P(("y", "z"), None, None),
            tokens,
        ),
        out_specs=(tokens, tokens),
        check_vma=False,
    )
```

```python
import functools

import jax
import jax.numpy as jnp
from jax import lax
from jax.experimental import pallas as pl
from jax.experimental.pallas import tpu as pltpu
from jax.sharding import Mesh, PartitionSpec as P

NY, NZ = 4, 8
GROUP = 4
FAR, NEAR = (2, 3, 4, 5), (6, 7, 0, 1)
CHUNK = 128
HEADS, HEAD = 8, 96
HD = HEADS * HEAD
TOK = 128
D = 1536
ROW = NZ * TOK
EXPERTS, CAP = 16, 32
CHAINS = 2
SLICE = 192
IDS = 16
F32, BF16 = jnp.float32, jnp.bfloat16
EXP2_SCALE = 1.4426950408889634 / HEAD**0.5
VMEM = pl.BlockSpec(memory_space=pltpu.VMEM)
NT = (((1,), (1,)), ((), ()))


def params(*semantics, mib=28):
    return pltpu.CompilerParams(
        dimension_semantics=semantics or None, vmem_limit_bytes=mib * 1024 * 1024
    )


def split_heads_kernel(*refs):
    ins, out_ref = refs[:-1], refs[-1]
    at = 0
    for ref in ins:
        turned = ref[...].astype(F32).T.astype(BF16)
        if turned.shape[0] < HD:
            for h in range(HEADS):
                out_ref[h, at : at + turned.shape[0], :] = turned
            at += turned.shape[0]
        for part in range(turned.shape[0] // HD):
            for h in range(HEADS):
                out_ref[h, at : at + HEAD, :] = turned[part * HD + h * HEAD : part * HD + (h + 1) * HEAD]
            at += HEAD


def split_heads(*arrays):
    rows = sum(a.shape[1] // HEADS if a.shape[1] >= HD else a.shape[1] for a in arrays)
    return pl.pallas_call(
        split_heads_kernel,
        out_shape=jax.ShapeDtypeStruct((HEADS, rows, TOK), BF16),
        in_specs=[VMEM] * len(arrays),
        out_specs=VMEM,
        compiler_params=params(),
    )(*arrays)


def update(q, kt, vt, state):
    s = jnp.dot(q, kt, preferred_element_type=F32)
    top = jnp.max(s, axis=1, keepdims=True)
    if state is not None:
        m, l, acc = state
        top = jnp.maximum(m, top)
    p = jnp.exp2((s - top) * EXP2_SCALE)
    total = jnp.sum(p, axis=1, keepdims=True)
    out = lax.dot_general(p.astype(BF16), vt, NT, preferred_element_type=F32)
    if state is not None:
        fade = jnp.exp2((m - top) * EXP2_SCALE)
        total, out = total + l * fade, out + acc * fade
    return top, total, out


def fill(refs, kt, vt):
    @pl.when(pl.program_id(0) == 0)
    def _():
        at = 0
        for ref in refs:
            for j in range(ref.shape[0]):
                kt[:, at : at + TOK] = ref[j, :HEAD]
                vt[:, at : at + TOK] = ref[j, HEAD : 2 * HEAD]
                at += TOK


STATE = 128


def unpack(ref):
    state = ref[...]
    return state[:, HEAD : HEAD + 1], state[:, HEAD + 1 : HEAD + 2], state[:, :HEAD]


def pack(ref, m, l, acc):
    ref[:, :HEAD] = acc
    ref[:, HEAD : HEAD + 1] = m
    ref[:, HEAD + 1 : HEAD + 2] = l


def own_row_kernel(own_ref, all_ref, q_ref, state_ref, kt, vt):
    i = pl.program_id(0)
    fill((all_ref,), kt, vt)
    cols = pl.ds(pl.multiple_of(i * TOK, TOK), TOK)
    kt[:, cols] = own_ref[0, 3 * HEAD : 4 * HEAD]
    vt[:, cols] = own_ref[0, 4 * HEAD : 5 * HEAD]
    q = own_ref[0, 2 * HEAD : 3 * HEAD].astype(F32).T.astype(BF16)
    q_ref[...] = q
    pack(state_ref, *update(q, kt[...], vt[...], None))
    kt[:, cols] = all_ref[i, :HEAD]
    vt[:, cols] = all_ref[i, HEAD : 2 * HEAD]


def attend_own_row(rows):
    return pl.pallas_call(
        own_row_kernel,
        grid=(NZ,),
        out_shape=(
            jax.ShapeDtypeStruct((ROW, HEAD), BF16),
            jax.ShapeDtypeStruct((ROW, STATE), F32),
        ),
        in_specs=[
            pl.BlockSpec((1,) + rows.shape[1:], lambda i: (i, 0, 0)),
            pl.BlockSpec((NZ, 2 * HEAD, TOK), lambda i: (0, 0, 0)),
        ],
        out_specs=(
            pl.BlockSpec((TOK, HEAD), lambda i: (i, 0)),
            pl.BlockSpec((TOK, STATE), lambda i: (i, 0)),
        ),
        scratch_shapes=[pltpu.VMEM((HEAD, ROW), BF16), pltpu.VMEM((HEAD, ROW), BF16)],
        compiler_params=params("arbitrary"),
        cost_estimate=pl.CostEstimate(
            flops=4 * ROW * ROW * HEAD, bytes_accessed=4 << 20, transcendentals=ROW * ROW
        ),
    )(rows, rows)


def other_rows_kernel(last, n, kvs, *refs):
    kv_refs, (q_ref, state_ref, out_ref, kt, vt) = refs[:kvs], refs[kvs:]
    fill(kv_refs, kt, vt)
    state = unpack(state_ref)
    for c in range(n):
        cols = slice(c * ROW, (c + 1) * ROW)
        state = update(q_ref[...], kt[:, cols], vt[:, cols], state)
    if last:
        out_ref[...] = (state[2] / state[1]).T.astype(BF16)
    else:
        pack(out_ref, *state)


def attend_other_rows(kvs, q, state, last, tile=512):
    n = sum(a.shape[0] for a in kvs) // NZ
    row = lambda width: pl.BlockSpec((tile, width), lambda i: (i, 0))
    if last:
        out_shape = jax.ShapeDtypeStruct((HEAD, ROW), BF16)
        out_specs = pl.BlockSpec((HEAD, tile), lambda i: (0, i))
    else:
        out_shape, out_specs = jax.ShapeDtypeStruct((ROW, STATE), F32), row(STATE)
    return pl.pallas_call(
        functools.partial(other_rows_kernel, last, n, len(kvs)),
        grid=(ROW // tile,),
        out_shape=out_shape,
        in_specs=[pl.BlockSpec(a.shape, lambda i: (0, 0, 0)) for a in kvs]
        + [row(HEAD), row(STATE)],
        out_specs=out_specs,
        scratch_shapes=[pltpu.VMEM((HEAD, n * ROW), BF16), pltpu.VMEM((HEAD, n * ROW), BF16)],
        compiler_params=params("arbitrary"),
        cost_estimate=pl.CostEstimate(
            flops=4 * ROW * n * ROW * HEAD, bytes_accessed=5 << 20, transcendentals=n * ROW * ROW
        ),
    )(*kvs, q, state)


def norm_kernel(own, pos, *refs):
    hid_refs, ids_refs, att_refs = refs[:GROUP], refs[GROUP : 2 * GROUP], refs[2 * GROUP : 3 * GROUP]
    wo_ref, mod_ref, rt_ref = refs[3 * GROUP : 3 * GROUP + 3]
    x_refs, g_ref, normed_ref = refs[3 * GROUP + 3 : 3 * GROUP + 3 + NY], refs[3 * GROUP + 3 + NY], refs[-1]
    if own is not None:
        res_ref, out_ref = refs[-3:-1]
    y, z = pos[0], pos[1]
    many = GROUP * TOK
    att = jnp.concatenate([ref[...] for ref in att_refs], axis=1).astype(F32).T.astype(BF16)
    scale, shift = 1.0 + mod_ref[0:1], mod_ref[1:2]
    for i in range(GROUP):
        for j in range(0, TOK, CHUNK):
            at = slice(i * TOK + j, i * TOK + j + CHUNK)
            resid = jnp.dot(att[at], wo_ref[...], preferred_element_type=F32)
            resid = resid + hid_refs[i][0, j : j + CHUNK].astype(F32)
            centered = resid - jnp.mean(resid, axis=1, keepdims=True)
            var = jnp.mean(centered * centered, axis=1, keepdims=True)
            normed_ref[at] = (centered * lax.rsqrt(var + 1e-06) * scale + shift).astype(BF16)
            if i == own:
                res_ref[j : j + CHUNK] = resid

    if own is not None:
        out_ref[...] = att[own * TOK : (own + 1) * TOK]

    normed = normed_ref[...]
    logits = jnp.dot(normed, rt_ref[...], preferred_element_type=F32)
    ids = jnp.concatenate([ref[0] for ref in ids_refs], axis=1).astype(F32).T.astype(jnp.int32)
    id0, id1 = ids[:, 0:1], ids[:, 1:2]
    lane = lax.broadcasted_iota(jnp.int32, (many, TOK), 1)
    zero = jnp.zeros((many, TOK), F32)
    logits = jnp.where(lane < 3 * EXPERTS, logits, zero)
    c0 = jnp.sum(jnp.where(lane % EXPERTS == id0, logits, zero), axis=1, keepdims=True)
    c1 = jnp.sum(jnp.where(lane % EXPERTS == id1, logits, zero), axis=1, keepdims=True)
    gate0 = jax.nn.sigmoid(c0 - c1)
    gate1 = 1.0 - gate0
    expert = ((y + lane // CAP) % NY) * NY + z // 2
    first, second = expert == id0, expert == id1
    chosen = jnp.where(first | second, 1.0, 0.0)
    gate = jnp.where(first, gate0, gate1)
    slot = (lane[:TOK] % CAP).astype(F32)
    token = lax.broadcasted_iota(jnp.int32, (TOK, TOK), 0)
    earlier = jnp.where(lane[:TOK] < token, 1.0, 0.0).astype(BF16)
    for i in range(GROUP):
        at = slice(i * TOK, (i + 1) * TOK)
        before = jnp.dot(earlier, chosen[at].astype(BF16), preferred_element_type=F32)
        hit = jnp.where(before == slot, chosen[at], 0.0)
        weight = hit * gate[at]
        high = weight.astype(BF16)
        g_ref[i, :, :TOK] = high
        g_ref[i, :, TOK:] = (weight - high.astype(F32)).astype(BF16)
        rows = jnp.dot(hit.T.astype(BF16), normed[at], preferred_element_type=F32).astype(BF16)
        for e in range(NY):
            x_refs[e][i] = rows[e * CAP : (e + 1) * CAP]


def norm_and_dispatch(blocks, pos, hid, att, w_out, modulation, router3, rows):
    n = len(blocks)
    own = 0 in blocks
    whole = lambda a: pl.BlockSpec(a.shape, lambda r, pos: (0,) * a.ndim)
    block = lambda i, r, pos: lax.rem(pos[1] + blocks[0] + r * GROUP + i, NZ)
    hids = [
        pl.BlockSpec((1, TOK, D), lambda r, pos, i=i: (block(i, r, pos), 0, 0)) for i in range(GROUP)
    ]
    ids = [
        pl.BlockSpec((1, IDS, TOK), lambda r, pos, i=i: (block(i, r, pos), 5 * HEAD // IDS, 0))
        for i in range(GROUP)
    ]
    atts = [pl.BlockSpec((HD, TOK), lambda r, pos, i=i: (0, block(i, r, pos))) for i in range(GROUP)]
    outs = [((n, CAP, D), BF16, (GROUP, CAP, D))] * NY + [((n, TOK, 2 * TOK), BF16, (GROUP, TOK, 2 * TOK))]
    if own:
        outs += [((TOK, D), F32, None), ((TOK, HD), BF16, None)]
    return pl.pallas_call(
        functools.partial(norm_kernel, blocks.index(0) if own else None),
        grid_spec=pltpu.PrefetchScalarGridSpec(
            num_scalar_prefetch=1,
            grid=(n // GROUP,),
            in_specs=hids + ids + atts + [whole(w_out), whole(modulation), whole(router3)],
            out_specs=tuple(
                pl.BlockSpec(tile, lambda r, pos: (r, 0, 0))
                if tile
                else pl.BlockSpec(shape, lambda r, pos: (0, 0))
                for shape, _, tile in outs
            ),
            scratch_shapes=[pltpu.VMEM((GROUP * TOK, D), BF16)],
        ),
        out_shape=tuple(jax.ShapeDtypeStruct(shape, t) for shape, t, _ in outs),
        compiler_params=params("arbitrary"),
        cost_estimate=pl.CostEstimate(
            flops=2 * n * TOK * D * (HD + 256), bytes_accessed=8 << 20, transcendentals=ROW
        ),
    )(pos, *[hid] * GROUP, *[rows] * GROUP, *[att] * GROUP, w_out, modulation, router3)


def expert_kernel(pick, tile, xa_ref, xb_ref, *refs):
    w_refs, (oa_ref, ob_ref, w1, w2, hidden, sems) = refs[:-6], refs[-6:]
    n = xa_ref.shape[0]
    steps = D // tile
    copies = []
    for p, held in enumerate((w1, w2)):
        for c in range(steps):
            cols = pl.ds(c * tile, tile)
            source = w_refs[0].at[:, p, :, cols] if pick else w_refs[p].at[:, :, cols]
            copy = pltpu.make_async_copy(source, held.at[:, :, cols], sems.at[p * steps + c])
            copy.start()
            copies.append(copy)
    x = jnp.concatenate([xa_ref[...], xb_ref[...]], axis=0)
    for c in range(steps):
        cols = slice(c * tile, (c + 1) * tile)
        copies[c].wait()
        first = jnp.dot(x, w1[:, :, cols].reshape(D, tile), preferred_element_type=F32)
        hidden[:, cols] = jax.nn.gelu(first, approximate=True).astype(BF16)
    for c in range(steps):
        cols = slice(c * tile, (c + 1) * tile)
        copies[steps + c].wait()
        out = jnp.dot(hidden[...], w2[:, :, cols].reshape(D, tile), preferred_element_type=F32)
        oa_ref[:, cols] = out[:n].astype(BF16)
        ob_ref[:, cols] = out[n:].astype(BF16)


def expert(xa, xb, *weights, tile=512):
    shape = xa.shape
    xa, xb = xa.reshape(-1, D), xb.reshape(-1, D)
    n = xa.shape[0]
    held = (D // SLICE, SLICE, D)
    pick = len(weights) == 1
    if not pick:
        weights = [w.reshape(held) for w in weights]
    ya, yb = pl.pallas_call(
        functools.partial(expert_kernel, pick, tile),
        out_shape=(jax.ShapeDtypeStruct((n, D), BF16),) * 2,
        in_specs=[VMEM, VMEM] + [pl.BlockSpec(memory_space=pl.ANY)] * len(weights),
        out_specs=(VMEM, VMEM),
        scratch_shapes=[
            pltpu.VMEM(held, BF16),
            pltpu.VMEM(held, BF16),
            pltpu.VMEM((2 * n, D), BF16),
            pltpu.SemaphoreType.DMA((2 * D // tile,)),
        ],
        compiler_params=params(mib=48),
        cost_estimate=pl.CostEstimate(
            flops=8 * n * D * D, bytes_accessed=11 << 20, transcendentals=2 * n * D
        ),
    )(xa, xb, *weights)
    return ya.reshape(shape), yb.reshape(shape)


def combine_kernel(blocks, *refs):
    g_ref, ys, outs = refs[0], refs[1:5], refs[5:]
    if 0 in blocks:
        res_ref, outs = outs[0], outs[1:]
    for i, block in enumerate(blocks):
        rows = jnp.concatenate([y[i] for y in ys], axis=0)
        total = jnp.dot(g_ref[i, :, :TOK], rows, preferred_element_type=F32)
        total = total + jnp.dot(g_ref[i, :, TOK:], rows, preferred_element_type=F32)
        if block == 0:
            total = total + res_ref[...]
        for c in range(CHAINS):
            out = outs[i * CHAINS + c]
            out[...] = total[:, c * D // CHAINS : (c + 1) * D // CHAINS].astype(out.dtype)


def combine(blocks, gates, ys, *resid):
    shapes = [
        jax.ShapeDtypeStruct((TOK, D // CHAINS), F32 if i == 0 else BF16)
        for i in blocks
        for _ in range(CHAINS)
    ]
    outs = pl.pallas_call(
        functools.partial(combine_kernel, blocks),
        out_shape=shapes,
        in_specs=[VMEM] * (5 + len(resid)),
        out_specs=[VMEM] * len(shapes),
        compiler_params=params(),
        cost_estimate=pl.CostEstimate(
            flops=4 * len(blocks) * TOK * TOK * D, bytes_accessed=4 << 20, transcendentals=0
        ),
    )(gates, *ys, *resid)
    return [
        {block: outs[i * CHAINS + c] for i, block in enumerate(blocks)} for c in range(CHAINS)
    ]


def send(x, axis, n, shift):
    return lax.ppermute(x, axis, [(i, (i + shift) % n) for i in range(n)])


def after(x, *done):
    return lax.optimization_barrier((x,) + done)[0]


def ring_z(x):
    got = [x] + [None] * (NZ - 1)
    up, down = x, x
    for s in range(1, 4):
        up, down = send(up, "z", NZ, 1), send(down, "z", NZ, -1)
        got[NZ - s], got[s] = up, down
    half = x.shape[0] // 2
    up, down = send(up[:half], "z", NZ, 1), send(down[half:], "z", NZ, -1)
    got[4] = jnp.concatenate([up, down], axis=0)
    return got


def in_order(blocks):
    z = lax.axis_index("z")
    out = jnp.zeros((NZ,) + blocks[0].shape, blocks[0].dtype)
    for r, block in enumerate(blocks):
        out = lax.dynamic_update_slice(out, block[None], ((z + r) % NZ, 0, 0))
    return out


def add(a, b):
    return (a.astype(F32) + b.astype(F32)).astype(BF16)


def scatter_first(parts):
    half = TOK // 2
    down, up = send(parts[4][:half], "z", NZ, -1), send(parts[4][half:], "z", NZ, 1)
    down = jnp.concatenate([add(parts[5][:half], down), parts[5][half:]], axis=0)
    up = jnp.concatenate([parts[3][:half], add(parts[3][half:], up)], axis=0)
    return lax.optimization_barrier((down, up))


def scatter_rest(parts, down, up):
    for s in (6, 7):
        down, up = send(down, "z", NZ, -1), send(up, "z", NZ, 1)
        down, up = add(parts[s], down), add(parts[NZ - s], up)
        down, up = lax.optimization_barrier((down, up))
    down, up = send(down, "z", NZ, -1), send(up, "z", NZ, 1)
    return (parts[0] + down.astype(F32) + up.astype(F32)).astype(BF16)


def per_device(
    hidden_in, queries, fresh_kv, stale_kv, modulation, w_out, router, fc_in, fc_out, expert_ids
):
    y, z = lax.axis_index("y"), lax.axis_index("z")
    pos = jnp.stack([y, z]).astype(jnp.int32)
    batch = lax.axis_size("batch")

    rows = D // batch
    w1, w2 = fc_in[0], fc_out[0]
    at = lax.axis_index("batch") * rows
    part = jnp.concatenate(
        [lax.dynamic_slice_in_dim(w, at, rows, 0) for w in (w1, w2)], axis=0
    )
    pieces, rest = [], router
    for _ in range(3):
        piece = lax.reduce_precision(rest, exponent_bits=8, mantissa_bits=7)
        rest = rest - piece
        pieces.append(piece.astype(BF16))
    router3 = jnp.pad(jnp.concatenate(pieces, axis=1), ((0, 0), (0, TOK - 3 * EXPERTS)))

    ids = jnp.pad(expert_ids.astype(BF16), ((0, 0), (0, IDS - 2)))
    heads = split_heads(after(stale_kv, part), queries, fresh_kv, ids)
    row = lax.all_to_all(heads, "z", split_axis=0, concat_axis=0, tiled=True)
    row, part_next, router3 = lax.optimization_barrier((row, send(part, "y", NY, -1), router3))
    hid = lax.all_gather(hidden_in, "z", axis=0, tiled=False)
    kv = row[:, : 2 * HEAD]
    kv_prev, kv_next = send(kv, "y", NY, 1), send(kv, "y", NY, -1)
    q, state = attend_own_row(row)
    kv_prev, kv_next, q = lax.optimization_barrier((kv_prev, kv_next, q))
    kv_far = [send(kv_prev[:4], "y", NY, 1), send(kv_next[4:], "y", NY, -1)]
    w_next = lax.all_gather(after(part_next, q), "batch", axis=0, tiled=False)
    w_next = w_next.reshape(batch, 2, rows, D)
    state = attend_other_rows([kv_prev, kv_next], q, state, False)
    att = attend_other_rows(kv_far, q, state, True)
    att = in_order(ring_z(att)).reshape(HD, ROW)

    groups = []
    for blocks in (FAR, NEAR):
        x0, x1, x2, x3, gates, *own = norm_and_dispatch(
            blocks, pos, hid, att, w_out, modulation, router3, row
        )
        att = after(att, x2)
        groups.append((blocks, x0, x1, send(x2, "y", NY, 1), send(x3, "y", NY, -1), gates, own))
    attended = own[1]

    ys, last = [], ()
    for _, x0, x1, x_prev, x_next, _, _ in groups:
        y0, y3 = expert(after(x0, *last), x_next, w1, w2)
        y1, y2 = expert(after(x1, y0), x_prev, w_next)
        ys.append((y0, y1, send(y2, "y", NY, -1), send(y3, "y", NY, 1)))
        last = (y1,)
    (_, *_, far_gates, _), (_, *_, near_gates, own) = groups
    far = combine(FAR, after(far_gates, *last), ys[0])
    sums = [scatter_first(parts) for parts in far]
    near = combine(NEAR, after(near_gates, *sums[0]), ys[1], own[0])
    mixed = [scatter_rest(far[c] | near[c], *sums[c]) for c in range(CHAINS)]
    return attended, jnp.concatenate(mixed, axis=1)


def solution(mesh):
    split = Mesh(mesh.devices.reshape(NY, NZ, -1), ("y", "z", "batch"))
    tokens = P(("batch", "y", "z"), None)
    return jax.shard_map(
        per_device,
        mesh=split,
        in_specs=(
            tokens,
            tokens,
            tokens,
            tokens,
            P("batch", None),
            P(),
            P(),
            P(("y", "z"), None, None),
            P(("y", "z"), None, None),
            tokens,
        ),
        out_specs=(tokens, tokens),
        check_vma=False,
    )
```

```python
import functools

import jax
import jax.numpy as jnp
from jax import lax
from jax.experimental import pallas as pl
from jax.experimental.pallas import tpu as pltpu
from jax.sharding import Mesh, PartitionSpec as P

NY, NZ = 4, 8
GROUP = 4
FAR, NEAR = (2, 3, 4, 5), (6, 7, 0, 1)
CHUNK = 128
HEADS, HEAD = 8, 96
HD = HEADS * HEAD
TOK = 128
D = 1536
ROW = NZ * TOK
EXPERTS, CAP = 16, 32
CHAINS = 2
SLICE = 192
IDS = 16
F32, BF16 = jnp.float32, jnp.bfloat16
EXP2_SCALE = 1.4426950408889634 / HEAD**0.5
VMEM = pl.BlockSpec(memory_space=pltpu.VMEM)
NT = (((1,), (1,)), ((), ()))


def params(*semantics, mib=28):
    return pltpu.CompilerParams(
        dimension_semantics=semantics or None, vmem_limit_bytes=mib * 1024 * 1024
    )


def split_heads_kernel(*refs):
    ins, out_ref = refs[:-1], refs[-1]
    at = 0
    for ref in ins:
        turned = ref[...].astype(F32).T.astype(BF16)
        if turned.shape[0] < HD:
            for h in range(HEADS):
                out_ref[h, at : at + turned.shape[0], :] = turned
            at += turned.shape[0]
        for part in range(turned.shape[0] // HD):
            for h in range(HEADS):
                out_ref[h, at : at + HEAD, :] = turned[part * HD + h * HEAD : part * HD + (h + 1) * HEAD]
            at += HEAD


def split_heads(*arrays):
    rows = sum(a.shape[1] // HEADS if a.shape[1] >= HD else a.shape[1] for a in arrays)
    return pl.pallas_call(
        split_heads_kernel,
        out_shape=jax.ShapeDtypeStruct((HEADS, rows, TOK), BF16),
        in_specs=[VMEM] * len(arrays),
        out_specs=VMEM,
        compiler_params=params(),
    )(*arrays)


def update(q, kt, vt, state):
    s = jnp.dot(q, kt, preferred_element_type=F32)
    top = jnp.max(s, axis=1, keepdims=True)
    if state is not None:
        m, l, acc = state
        top = jnp.maximum(m, top)
    p = jnp.exp2((s - top) * EXP2_SCALE)
    total = jnp.sum(p, axis=1, keepdims=True)
    out = lax.dot_general(p.astype(BF16), vt, NT, preferred_element_type=F32)
    if state is not None:
        fade = jnp.exp2((m - top) * EXP2_SCALE)
        total, out = total + l * fade, out + acc * fade
    return top, total, out


def fill(refs, kt, vt):
    @pl.when(pl.program_id(0) == 0)
    def _():
        at = 0
        for ref in refs:
            for j in range(ref.shape[0]):
                kt[:, at : at + TOK] = ref[j, :HEAD]
                vt[:, at : at + TOK] = ref[j, HEAD : 2 * HEAD]
                at += TOK


STATE = 128


def unpack(ref):
    state = ref[...]
    return state[:, HEAD : HEAD + 1], state[:, HEAD + 1 : HEAD + 2], state[:, :HEAD]


def pack(ref, m, l, acc):
    ref[:, :HEAD] = acc
    ref[:, HEAD : HEAD + 1] = m
    ref[:, HEAD + 1 : HEAD + 2] = l


def own_row_kernel(own_ref, all_ref, q_ref, state_ref, kt, vt):
    i = pl.program_id(0)
    fill((all_ref,), kt, vt)
    cols = pl.ds(pl.multiple_of(i * TOK, TOK), TOK)
    kt[:, cols] = own_ref[0, 3 * HEAD : 4 * HEAD]
    vt[:, cols] = own_ref[0, 4 * HEAD : 5 * HEAD]
    q = own_ref[0, 2 * HEAD : 3 * HEAD].astype(F32).T.astype(BF16)
    q_ref[...] = q
    pack(state_ref, *update(q, kt[...], vt[...], None))
    kt[:, cols] = all_ref[i, :HEAD]
    vt[:, cols] = all_ref[i, HEAD : 2 * HEAD]


def attend_own_row(rows):
    return pl.pallas_call(
        own_row_kernel,
        grid=(NZ,),
        out_shape=(
            jax.ShapeDtypeStruct((ROW, HEAD), BF16),
            jax.ShapeDtypeStruct((ROW, STATE), F32),
        ),
        in_specs=[
            pl.BlockSpec((1,) + rows.shape[1:], lambda i: (i, 0, 0)),
            pl.BlockSpec((NZ, 2 * HEAD, TOK), lambda i: (0, 0, 0)),
        ],
        out_specs=(
            pl.BlockSpec((TOK, HEAD), lambda i: (i, 0)),
            pl.BlockSpec((TOK, STATE), lambda i: (i, 0)),
        ),
        scratch_shapes=[pltpu.VMEM((HEAD, ROW), BF16), pltpu.VMEM((HEAD, ROW), BF16)],
        compiler_params=params("arbitrary"),
        cost_estimate=pl.CostEstimate(
            flops=4 * ROW * ROW * HEAD, bytes_accessed=4 << 20, transcendentals=ROW * ROW
        ),
    )(rows, rows)


def other_rows_kernel(last, n, kvs, *refs):
    kv_refs, (q_ref, state_ref, out_ref, kt, vt) = refs[:kvs], refs[kvs:]
    fill(kv_refs, kt, vt)
    state = unpack(state_ref)
    for c in range(n):
        cols = slice(c * ROW, (c + 1) * ROW)
        state = update(q_ref[...], kt[:, cols], vt[:, cols], state)
    if last:
        out_ref[...] = (state[2] / state[1]).T.astype(BF16)
    else:
        pack(out_ref, *state)


def attend_other_rows(kvs, q, state, last, tile=512):
    n = sum(a.shape[0] for a in kvs) // NZ
    row = lambda width: pl.BlockSpec((tile, width), lambda i: (i, 0))
    if last:
        out_shape = jax.ShapeDtypeStruct((HEAD, ROW), BF16)
        out_specs = pl.BlockSpec((HEAD, tile), lambda i: (0, i))
    else:
        out_shape, out_specs = jax.ShapeDtypeStruct((ROW, STATE), F32), row(STATE)
    return pl.pallas_call(
        functools.partial(other_rows_kernel, last, n, len(kvs)),
        grid=(ROW // tile,),
        out_shape=out_shape,
        in_specs=[pl.BlockSpec(a.shape, lambda i: (0, 0, 0)) for a in kvs]
        + [row(HEAD), row(STATE)],
        out_specs=out_specs,
        scratch_shapes=[pltpu.VMEM((HEAD, n * ROW), BF16), pltpu.VMEM((HEAD, n * ROW), BF16)],
        compiler_params=params("arbitrary"),
        cost_estimate=pl.CostEstimate(
            flops=4 * ROW * n * ROW * HEAD, bytes_accessed=5 << 20, transcendentals=n * ROW * ROW
        ),
    )(*kvs, q, state)


def norm_kernel(own, pos, *refs):
    hid_refs, ids_refs, att_refs = refs[:GROUP], refs[GROUP : 2 * GROUP], refs[2 * GROUP : 3 * GROUP]
    wo_ref, mod_ref, rt_ref = refs[3 * GROUP : 3 * GROUP + 3]
    x_refs, g_ref, normed_ref = refs[3 * GROUP + 3 : 3 * GROUP + 3 + NY], refs[3 * GROUP + 3 + NY], refs[-1]
    if own is not None:
        res_ref, out_ref = refs[-3:-1]
    y, z = pos[0], pos[1]
    many = GROUP * TOK
    att = jnp.concatenate([ref[...] for ref in att_refs], axis=1).astype(F32).T.astype(BF16)
    scale, shift = 1.0 + mod_ref[0:1], mod_ref[1:2]
    for i in range(GROUP):
        for j in range(0, TOK, CHUNK):
            at = slice(i * TOK + j, i * TOK + j + CHUNK)
            resid = jnp.dot(att[at], wo_ref[...], preferred_element_type=F32)
            resid = resid + hid_refs[i][0, j : j + CHUNK].astype(F32)
            centered = resid - jnp.mean(resid, axis=1, keepdims=True)
            var = jnp.mean(centered * centered, axis=1, keepdims=True)
            normed_ref[at] = (centered * lax.rsqrt(var + 1e-06) * scale + shift).astype(BF16)
            if i == own:
                res_ref[j : j + CHUNK] = resid

    if own is not None:
        out_ref[...] = att[own * TOK : (own + 1) * TOK]

    normed = normed_ref[...]
    logits = jnp.dot(normed, rt_ref[...], preferred_element_type=F32)
    ids = jnp.concatenate([ref[0] for ref in ids_refs], axis=1).astype(F32).T.astype(jnp.int32)
    id0, id1 = ids[:, 0:1], ids[:, 1:2]
    lane = lax.broadcasted_iota(jnp.int32, (many, TOK), 1)
    zero = jnp.zeros((many, TOK), F32)
    logits = jnp.where(lane < 3 * EXPERTS, logits, zero)
    c0 = jnp.sum(jnp.where(lane % EXPERTS == id0, logits, zero), axis=1, keepdims=True)
    c1 = jnp.sum(jnp.where(lane % EXPERTS == id1, logits, zero), axis=1, keepdims=True)
    gate0 = jax.nn.sigmoid(c0 - c1)
    gate1 = 1.0 - gate0
    expert = ((y + lane // CAP) % NY) * NY + z // 2
    first, second = expert == id0, expert == id1
    chosen = jnp.where(first | second, 1.0, 0.0)
    gate = jnp.where(first, gate0, gate1)
    slot = (lane[:TOK] % CAP).astype(F32)
    token = lax.broadcasted_iota(jnp.int32, (TOK, TOK), 0)
    earlier = jnp.where(lane[:TOK] < token, 1.0, 0.0).astype(BF16)
    for i in range(GROUP):
        at = slice(i * TOK, (i + 1) * TOK)
        before = jnp.dot(earlier, chosen[at].astype(BF16), preferred_element_type=F32)
        hit = jnp.where(before == slot, chosen[at], 0.0)
        weight = hit * gate[at]
        high = weight.astype(BF16)
        g_ref[i, :, :TOK] = high
        g_ref[i, :, TOK:] = (weight - high.astype(F32)).astype(BF16)
        rows = jnp.dot(hit.T.astype(BF16), normed[at], preferred_element_type=F32).astype(BF16)
        for e in range(NY):
            x_refs[e][i] = rows[e * CAP : (e + 1) * CAP]


def norm_and_dispatch(blocks, pos, hid, att, w_out, modulation, router3, rows):
    n = len(blocks)
    own = 0 in blocks
    whole = lambda a: pl.BlockSpec(a.shape, lambda r, pos: (0,) * a.ndim)
    block = lambda i, r, pos: lax.rem(pos[1] + blocks[0] + r * GROUP + i, NZ)
    hids = [
        pl.BlockSpec((1, TOK, D), lambda r, pos, i=i: (block(i, r, pos), 0, 0)) for i in range(GROUP)
    ]
    ids = [
        pl.BlockSpec((1, IDS, TOK), lambda r, pos, i=i: (block(i, r, pos), 5 * HEAD // IDS, 0))
        for i in range(GROUP)
    ]
    atts = [pl.BlockSpec((HD, TOK), lambda r, pos, i=i: (0, block(i, r, pos))) for i in range(GROUP)]
    outs = [((n, CAP, D), BF16, (GROUP, CAP, D))] * NY + [((n, TOK, 2 * TOK), BF16, (GROUP, TOK, 2 * TOK))]
    if own:
        outs += [((TOK, D), F32, None), ((TOK, HD), BF16, None)]
    return pl.pallas_call(
        functools.partial(norm_kernel, blocks.index(0) if own else None),
        grid_spec=pltpu.PrefetchScalarGridSpec(
            num_scalar_prefetch=1,
            grid=(n // GROUP,),
            in_specs=hids + ids + atts + [whole(w_out), whole(modulation), whole(router3)],
            out_specs=tuple(
                pl.BlockSpec(tile, lambda r, pos: (r, 0, 0))
                if tile
                else pl.BlockSpec(shape, lambda r, pos: (0, 0))
                for shape, _, tile in outs
            ),
            scratch_shapes=[pltpu.VMEM((GROUP * TOK, D), BF16)],
        ),
        out_shape=tuple(jax.ShapeDtypeStruct(shape, t) for shape, t, _ in outs),
        compiler_params=params("arbitrary"),
        cost_estimate=pl.CostEstimate(
            flops=2 * n * TOK * D * (HD + 256), bytes_accessed=8 << 20, transcendentals=ROW
        ),
    )(pos, *[hid] * GROUP, *[rows] * GROUP, *[att] * GROUP, w_out, modulation, router3)


def expert_kernel(pick, tile, xa_ref, xb_ref, *refs):
    w_refs, (oa_ref, ob_ref, w1, w2, hidden, sems) = refs[:-6], refs[-6:]
    n = xa_ref.shape[0]
    steps = D // tile
    copies = []
    for p, held in enumerate((w1, w2)):
        for c in range(steps):
            cols = pl.ds(c * tile, tile)
            source = w_refs[0].at[:, p, :, cols] if pick else w_refs[p].at[:, :, cols]
            copy = pltpu.make_async_copy(source, held.at[:, :, cols], sems.at[p * steps + c])
            copy.start()
            copies.append(copy)
    x = jnp.concatenate([xa_ref[...], xb_ref[...]], axis=0)
    for c in range(steps):
        cols = slice(c * tile, (c + 1) * tile)
        copies[c].wait()
        first = jnp.dot(x, w1[:, :, cols].reshape(D, tile), preferred_element_type=F32)
        hidden[:, cols] = jax.nn.gelu(first, approximate=True).astype(BF16)
    for c in range(steps):
        cols = slice(c * tile, (c + 1) * tile)
        copies[steps + c].wait()
        out = jnp.dot(hidden[...], w2[:, :, cols].reshape(D, tile), preferred_element_type=F32)
        oa_ref[:, cols] = out[:n].astype(BF16)
        ob_ref[:, cols] = out[n:].astype(BF16)


def expert(xa, xb, *weights, tile=512):
    shape = xa.shape
    xa, xb = xa.reshape(-1, D), xb.reshape(-1, D)
    n = xa.shape[0]
    held = (D // SLICE, SLICE, D)
    pick = len(weights) == 1
    if not pick:
        weights = [w.reshape(held) for w in weights]
    ya, yb = pl.pallas_call(
        functools.partial(expert_kernel, pick, tile),
        out_shape=(jax.ShapeDtypeStruct((n, D), BF16),) * 2,
        in_specs=[VMEM, VMEM] + [pl.BlockSpec(memory_space=pl.ANY)] * len(weights),
        out_specs=(VMEM, VMEM),
        scratch_shapes=[
            pltpu.VMEM(held, BF16),
            pltpu.VMEM(held, BF16),
            pltpu.VMEM((2 * n, D), BF16),
            pltpu.SemaphoreType.DMA((2 * D // tile,)),
        ],
        compiler_params=params(mib=48),
        cost_estimate=pl.CostEstimate(
            flops=8 * n * D * D, bytes_accessed=11 << 20, transcendentals=2 * n * D
        ),
    )(xa, xb, *weights)
    return ya.reshape(shape), yb.reshape(shape)


def combine_kernel(blocks, *refs):
    g_ref, ys, outs = refs[0], refs[1:5], refs[5:]
    if 0 in blocks:
        res_ref, outs = outs[0], outs[1:]
    for i, block in enumerate(blocks):
        rows = jnp.concatenate([y[i] for y in ys], axis=0)
        total = jnp.dot(g_ref[i, :, :TOK], rows, preferred_element_type=F32)
        total = total + jnp.dot(g_ref[i, :, TOK:], rows, preferred_element_type=F32)
        if block == 0:
            total = total + res_ref[...]
        for c in range(CHAINS):
            out = outs[i * CHAINS + c]
            out[...] = total[:, c * D // CHAINS : (c + 1) * D // CHAINS].astype(out.dtype)


def combine(blocks, gates, ys, *resid):
    shapes = [
        jax.ShapeDtypeStruct((TOK, D // CHAINS), F32 if i == 0 else BF16)
        for i in blocks
        for _ in range(CHAINS)
    ]
    outs = pl.pallas_call(
        functools.partial(combine_kernel, blocks),
        out_shape=shapes,
        in_specs=[VMEM] * (5 + len(resid)),
        out_specs=[VMEM] * len(shapes),
        compiler_params=params(),
        cost_estimate=pl.CostEstimate(
            flops=4 * len(blocks) * TOK * TOK * D, bytes_accessed=4 << 20, transcendentals=0
        ),
    )(gates, *ys, *resid)
    return [
        {block: outs[i * CHAINS + c] for i, block in enumerate(blocks)} for c in range(CHAINS)
    ]


def send(x, axis, n, shift):
    return lax.ppermute(x, axis, [(i, (i + shift) % n) for i in range(n)])


def after(x, *done):
    return lax.optimization_barrier((x,) + done)[0]


def ring_z(x):
    got = [x] + [None] * (NZ - 1)
    up, down = x, x
    for s in range(1, 4):
        up, down = send(up, "z", NZ, 1), send(down, "z", NZ, -1)
        got[NZ - s], got[s] = up, down
    half = x.shape[0] // 2
    up, down = send(up[:half], "z", NZ, 1), send(down[half:], "z", NZ, -1)
    got[4] = jnp.concatenate([up, down], axis=0)
    return got


def in_order(blocks):
    z = lax.axis_index("z")
    out = jnp.zeros((NZ,) + blocks[0].shape, blocks[0].dtype)
    for r, block in enumerate(blocks):
        out = lax.dynamic_update_slice(out, block[None], ((z + r) % NZ, 0, 0))
    return out


def add(a, b):
    return (a.astype(F32) + b.astype(F32)).astype(BF16)


def scatter_first(parts):
    half = TOK // 2
    down, up = send(parts[4][:half], "z", NZ, -1), send(parts[4][half:], "z", NZ, 1)
    down = jnp.concatenate([add(parts[5][:half], down), parts[5][half:]], axis=0)
    up = jnp.concatenate([parts[3][:half], add(parts[3][half:], up)], axis=0)
    return lax.optimization_barrier((down, up))


def scatter_rest(parts, down, up):
    for s in (6, 7):
        down, up = send(down, "z", NZ, -1), send(up, "z", NZ, 1)
        down, up = add(parts[s], down), add(parts[NZ - s], up)
    down, up = send(down, "z", NZ, -1), send(up, "z", NZ, 1)
    return (parts[0] + down.astype(F32) + up.astype(F32)).astype(BF16)


def per_device(
    hidden_in, queries, fresh_kv, stale_kv, modulation, w_out, router, fc_in, fc_out, expert_ids
):
    y, z = lax.axis_index("y"), lax.axis_index("z")
    pos = jnp.stack([y, z]).astype(jnp.int32)
    batch = lax.axis_size("batch")

    rows = D // batch
    w1, w2 = fc_in[0], fc_out[0]
    at = lax.axis_index("batch") * rows
    part = jnp.concatenate(
        [lax.dynamic_slice_in_dim(w, at, rows, 0) for w in (w1, w2)], axis=0
    )
    pieces, rest = [], router
    for _ in range(3):
        piece = lax.reduce_precision(rest, exponent_bits=8, mantissa_bits=7)
        rest = rest - piece
        pieces.append(piece.astype(BF16))
    router3 = jnp.pad(jnp.concatenate(pieces, axis=1), ((0, 0), (0, TOK - 3 * EXPERTS)))

    ids = jnp.pad(expert_ids.astype(BF16), ((0, 0), (0, IDS - 2)))
    heads = split_heads(after(stale_kv, part), queries, fresh_kv, ids)
    row = lax.all_to_all(heads, "z", split_axis=0, concat_axis=0, tiled=True)
    row, part_next, router3 = lax.optimization_barrier((row, send(part, "y", NY, -1), router3))
    hid = lax.all_gather(hidden_in, "z", axis=0, tiled=False)
    kv = row[:, : 2 * HEAD]
    kv_prev, kv_next = send(kv, "y", NY, 1), send(kv, "y", NY, -1)
    q, state = attend_own_row(row)
    kv_prev, kv_next, q = lax.optimization_barrier((kv_prev, kv_next, q))
    kv_far = [send(kv_prev[:4], "y", NY, 1), send(kv_next[4:], "y", NY, -1)]
    w_next = lax.all_gather(after(part_next, q), "batch", axis=0, tiled=False)
    w_next = w_next.reshape(batch, 2, rows, D)
    state = attend_other_rows([kv_prev, kv_next], q, state, False)
    att = attend_other_rows(kv_far, q, state, True)
    att = in_order(ring_z(att)).reshape(HD, ROW)

    groups = []
    for blocks in (FAR, NEAR):
        x0, x1, x2, x3, gates, *own = norm_and_dispatch(
            blocks, pos, hid, att, w_out, modulation, router3, row
        )
        att = after(att, x2)
        groups.append((blocks, x0, x1, send(x2, "y", NY, 1), send(x3, "y", NY, -1), gates, own))
    attended = own[1]

    ys, last = [], ()
    for _, x0, x1, x_prev, x_next, _, _ in groups:
        y0, y3 = expert(after(x0, *last), x_next, w1, w2)
        y1, y2 = expert(after(x1, y0), x_prev, w_next)
        ys.append((y0, y1, send(y2, "y", NY, -1), send(y3, "y", NY, 1)))
        last = (y1,)
    (_, *_, far_gates, _), (_, *_, near_gates, own) = groups
    far = combine(FAR, after(far_gates, *last), ys[0])
    sums = [scatter_first(parts) for parts in far]
    near = combine(NEAR, after(near_gates, *sums[0], *sums[1]), ys[1], own[0])
    mixed = [scatter_rest(far[c] | near[c], *sums[c]) for c in range(CHAINS)]
    return attended, jnp.concatenate(mixed, axis=1)


def solution(mesh):
    split = Mesh(mesh.devices.reshape(NY, NZ, -1), ("y", "z", "batch"))
    tokens = P(("batch", "y", "z"), None)
    return jax.shard_map(
        per_device,
        mesh=split,
        in_specs=(
            tokens,
            tokens,
            tokens,
            tokens,
            P("batch", None),
            P(),
            P(),
            P(("y", "z"), None, None),
            P(("y", "z"), None, None),
            tokens,
        ),
        out_specs=(tokens, tokens),
        check_vma=False,
    )
```

```python
import functools

import jax
import jax.numpy as jnp
from jax import lax
from jax.experimental import pallas as pl
from jax.experimental.pallas import tpu as pltpu
from jax.sharding import Mesh, PartitionSpec as P

NY, NZ = 4, 8
GROUP = 4
FAR, NEAR = (2, 3, 4, 5), (6, 7, 0, 1)
CHUNK = 128
HEADS, HEAD = 8, 96
HD = HEADS * HEAD
TOK = 128
D = 1536
ROW = NZ * TOK
EXPERTS, CAP = 16, 32
CHAINS = 2
SLICE = 192
IDS = 16
F32, BF16 = jnp.float32, jnp.bfloat16
EXP2_SCALE = 1.4426950408889634 / HEAD**0.5
VMEM = pl.BlockSpec(memory_space=pltpu.VMEM)
NT = (((1,), (1,)), ((), ()))


def params(*semantics, mib=28):
    return pltpu.CompilerParams(
        dimension_semantics=semantics or None, vmem_limit_bytes=mib * 1024 * 1024
    )


def split_heads_kernel(*refs):
    ins, out_ref = refs[:-1], refs[-1]
    at = 0
    for ref in ins:
        turned = ref[...].astype(F32).T.astype(BF16)
        if turned.shape[0] < HD:
            for h in range(HEADS):
                out_ref[h, at : at + turned.shape[0], :] = turned
            at += turned.shape[0]
        for part in range(turned.shape[0] // HD):
            for h in range(HEADS):
                out_ref[h, at : at + HEAD, :] = turned[part * HD + h * HEAD : part * HD + (h + 1) * HEAD]
            at += HEAD


def split_heads(*arrays):
    rows = sum(a.shape[1] // HEADS if a.shape[1] >= HD else a.shape[1] for a in arrays)
    return pl.pallas_call(
        split_heads_kernel,
        out_shape=jax.ShapeDtypeStruct((HEADS, rows, TOK), BF16),
        in_specs=[VMEM] * len(arrays),
        out_specs=VMEM,
        compiler_params=params(),
    )(*arrays)


def update(q, kt, vt, state):
    s = jnp.dot(q, kt, preferred_element_type=F32)
    top = jnp.max(s, axis=1, keepdims=True)
    if state is not None:
        m, l, acc = state
        top = jnp.maximum(m, top)
    p = jnp.exp2((s - top) * EXP2_SCALE)
    total = jnp.sum(p, axis=1, keepdims=True)
    out = lax.dot_general(p.astype(BF16), vt, NT, preferred_element_type=F32)
    if state is not None:
        fade = jnp.exp2((m - top) * EXP2_SCALE)
        total, out = total + l * fade, out + acc * fade
    return top, total, out


def fill(refs, kt, vt):
    @pl.when(pl.program_id(0) == 0)
    def _():
        at = 0
        for ref in refs:
            for j in range(ref.shape[0]):
                kt[:, at : at + TOK] = ref[j, :HEAD]
                vt[:, at : at + TOK] = ref[j, HEAD : 2 * HEAD]
                at += TOK


STATE = 128


def unpack(ref):
    state = ref[...]
    return state[:, HEAD : HEAD + 1], state[:, HEAD + 1 : HEAD + 2], state[:, :HEAD]


def pack(ref, m, l, acc):
    ref[:, :HEAD] = acc
    ref[:, HEAD : HEAD + 1] = m
    ref[:, HEAD + 1 : HEAD + 2] = l


def own_row_kernel(own_ref, all_ref, q_ref, state_ref, kt, vt):
    i = pl.program_id(0)
    fill((all_ref,), kt, vt)
    cols = pl.ds(pl.multiple_of(i * TOK, TOK), TOK)
    kt[:, cols] = own_ref[0, 3 * HEAD : 4 * HEAD]
    vt[:, cols] = own_ref[0, 4 * HEAD : 5 * HEAD]
    q = own_ref[0, 2 * HEAD : 3 * HEAD].astype(F32).T.astype(BF16)
    q_ref[...] = q
    pack(state_ref, *update(q, kt[...], vt[...], None))
    kt[:, cols] = all_ref[i, :HEAD]
    vt[:, cols] = all_ref[i, HEAD : 2 * HEAD]


def attend_own_row(rows):
    return pl.pallas_call(
        own_row_kernel,
        grid=(NZ,),
        out_shape=(
            jax.ShapeDtypeStruct((ROW, HEAD), BF16),
            jax.ShapeDtypeStruct((ROW, STATE), F32),
        ),
        in_specs=[
            pl.BlockSpec((1,) + rows.shape[1:], lambda i: (i, 0, 0)),
            pl.BlockSpec((NZ, 2 * HEAD, TOK), lambda i: (0, 0, 0)),
        ],
        out_specs=(
            pl.BlockSpec((TOK, HEAD), lambda i: (i, 0)),
            pl.BlockSpec((TOK, STATE), lambda i: (i, 0)),
        ),
        scratch_shapes=[pltpu.VMEM((HEAD, ROW), BF16), pltpu.VMEM((HEAD, ROW), BF16)],
        compiler_params=params("arbitrary"),
        cost_estimate=pl.CostEstimate(
            flops=4 * ROW * ROW * HEAD, bytes_accessed=4 << 20, transcendentals=ROW * ROW
        ),
    )(rows, rows)


def other_rows_kernel(last, n, kvs, *refs):
    kv_refs, (q_ref, state_ref, out_ref, kt, vt) = refs[:kvs], refs[kvs:]
    fill(kv_refs, kt, vt)
    state = unpack(state_ref)
    for c in range(n):
        cols = slice(c * ROW, (c + 1) * ROW)
        state = update(q_ref[...], kt[:, cols], vt[:, cols], state)
    if last:
        out_ref[...] = (state[2] / state[1]).T.astype(BF16)
    else:
        pack(out_ref, *state)


def attend_other_rows(kvs, q, state, last, tile=512):
    n = sum(a.shape[0] for a in kvs) // NZ
    row = lambda width: pl.BlockSpec((tile, width), lambda i: (i, 0))
    if last:
        out_shape = jax.ShapeDtypeStruct((HEAD, ROW), BF16)
        out_specs = pl.BlockSpec((HEAD, tile), lambda i: (0, i))
    else:
        out_shape, out_specs = jax.ShapeDtypeStruct((ROW, STATE), F32), row(STATE)
    return pl.pallas_call(
        functools.partial(other_rows_kernel, last, n, len(kvs)),
        grid=(ROW // tile,),
        out_shape=out_shape,
        in_specs=[pl.BlockSpec(a.shape, lambda i: (0, 0, 0)) for a in kvs]
        + [row(HEAD), row(STATE)],
        out_specs=out_specs,
        scratch_shapes=[pltpu.VMEM((HEAD, n * ROW), BF16), pltpu.VMEM((HEAD, n * ROW), BF16)],
        compiler_params=params("arbitrary"),
        cost_estimate=pl.CostEstimate(
            flops=4 * ROW * n * ROW * HEAD, bytes_accessed=5 << 20, transcendentals=n * ROW * ROW
        ),
    )(*kvs, q, state)


def norm_kernel(own, pos, *refs):
    hid_refs, ids_refs, att_refs = refs[:GROUP], refs[GROUP : 2 * GROUP], refs[2 * GROUP : 3 * GROUP]
    wo_ref, mod_ref, rt_ref = refs[3 * GROUP : 3 * GROUP + 3]
    x_refs, g_ref, normed_ref = refs[3 * GROUP + 3 : 3 * GROUP + 3 + NY], refs[3 * GROUP + 3 + NY], refs[-1]
    if own is not None:
        res_ref, out_ref = refs[-3:-1]
    y, z = pos[0], pos[1]
    many = GROUP * TOK
    att = jnp.concatenate([ref[...] for ref in att_refs], axis=1).astype(F32).T.astype(BF16)
    scale, shift = 1.0 + mod_ref[0:1], mod_ref[1:2]
    for i in range(GROUP):
        for j in range(0, TOK, CHUNK):
            at = slice(i * TOK + j, i * TOK + j + CHUNK)
            resid = jnp.dot(att[at], wo_ref[...], preferred_element_type=F32)
            resid = resid + hid_refs[i][0, j : j + CHUNK].astype(F32)
            centered = resid - jnp.mean(resid, axis=1, keepdims=True)
            var = jnp.mean(centered * centered, axis=1, keepdims=True)
            normed_ref[at] = (centered * lax.rsqrt(var + 1e-06) * scale + shift).astype(BF16)
            if i == own:
                res_ref[j : j + CHUNK] = resid

    if own is not None:
        out_ref[...] = att[own * TOK : (own + 1) * TOK]

    normed = normed_ref[...]
    logits = jnp.dot(normed, rt_ref[...], preferred_element_type=F32)
    ids = jnp.concatenate([ref[0] for ref in ids_refs], axis=1).astype(F32).T.astype(jnp.int32)
    id0, id1 = ids[:, 0:1], ids[:, 1:2]
    lane = lax.broadcasted_iota(jnp.int32, (many, TOK), 1)
    zero = jnp.zeros((many, TOK), F32)
    logits = jnp.where(lane < 3 * EXPERTS, logits, zero)
    c0 = jnp.sum(jnp.where(lane % EXPERTS == id0, logits, zero), axis=1, keepdims=True)
    c1 = jnp.sum(jnp.where(lane % EXPERTS == id1, logits, zero), axis=1, keepdims=True)
    gate0 = jax.nn.sigmoid(c0 - c1)
    gate1 = 1.0 - gate0
    expert = ((y + lane // CAP) % NY) * NY + z // 2
    first, second = expert == id0, expert == id1
    chosen = jnp.where(first | second, 1.0, 0.0)
    gate = jnp.where(first, gate0, gate1)
    slot = (lane[:TOK] % CAP).astype(F32)
    token = lax.broadcasted_iota(jnp.int32, (TOK, TOK), 0)
    earlier = jnp.where(lane[:TOK] < token, 1.0, 0.0).astype(BF16)
    for i in range(GROUP):
        at = slice(i * TOK, (i + 1) * TOK)
        before = jnp.dot(earlier, chosen[at].astype(BF16), preferred_element_type=F32)
        hit = jnp.where(before == slot, chosen[at], 0.0)
        weight = hit * gate[at]
        high = weight.astype(BF16)
        g_ref[i, :, :TOK] = high
        g_ref[i, :, TOK:] = (weight - high.astype(F32)).astype(BF16)
        rows = jnp.dot(hit.T.astype(BF16), normed[at], preferred_element_type=F32).astype(BF16)
        for e in range(NY):
            x_refs[e][i] = rows[e * CAP : (e + 1) * CAP]


def norm_and_dispatch(blocks, pos, hid, att, w_out, modulation, router3, rows):
    n = len(blocks)
    own = 0 in blocks
    whole = lambda a: pl.BlockSpec(a.shape, lambda r, pos: (0,) * a.ndim)
    block = lambda i, r, pos: lax.rem(pos[1] + blocks[0] + r * GROUP + i, NZ)
    hids = [
        pl.BlockSpec((1, TOK, D), lambda r, pos, i=i: (block(i, r, pos), 0, 0)) for i in range(GROUP)
    ]
    ids = [
        pl.BlockSpec((1, IDS, TOK), lambda r, pos, i=i: (block(i, r, pos), 5 * HEAD // IDS, 0))
        for i in range(GROUP)
    ]
    atts = [pl.BlockSpec((HD, TOK), lambda r, pos, i=i: (0, block(i, r, pos))) for i in range(GROUP)]
    outs = [((n, CAP, D), BF16, (GROUP, CAP, D))] * NY + [((n, TOK, 2 * TOK), BF16, (GROUP, TOK, 2 * TOK))]
    if own:
        outs += [((TOK, D), F32, None), ((TOK, HD), BF16, None)]
    return pl.pallas_call(
        functools.partial(norm_kernel, blocks.index(0) if own else None),
        grid_spec=pltpu.PrefetchScalarGridSpec(
            num_scalar_prefetch=1,
            grid=(n // GROUP,),
            in_specs=hids + ids + atts + [whole(w_out), whole(modulation), whole(router3)],
            out_specs=tuple(
                pl.BlockSpec(tile, lambda r, pos: (r, 0, 0))
                if tile
                else pl.BlockSpec(shape, lambda r, pos: (0, 0))
                for shape, _, tile in outs
            ),
            scratch_shapes=[pltpu.VMEM((GROUP * TOK, D), BF16)],
        ),
        out_shape=tuple(jax.ShapeDtypeStruct(shape, t) for shape, t, _ in outs),
        compiler_params=params("arbitrary"),
        cost_estimate=pl.CostEstimate(
            flops=2 * n * TOK * D * (HD + 256), bytes_accessed=8 << 20, transcendentals=ROW
        ),
    )(pos, *[hid] * GROUP, *[rows] * GROUP, *[att] * GROUP, w_out, modulation, router3)


def expert_kernel(pick, tile, xa_ref, xb_ref, *refs):
    w_refs, (oa_ref, ob_ref, w1, w2, hidden, sems) = refs[:-6], refs[-6:]
    n = xa_ref.shape[0]
    steps = D // tile
    copies = []
    for p, held in enumerate((w1, w2)):
        for c in range(steps):
            cols = pl.ds(c * tile, tile)
            source = w_refs[0].at[:, p, :, cols] if pick else w_refs[p].at[:, :, cols]
            copy = pltpu.make_async_copy(source, held.at[:, :, cols], sems.at[p * steps + c])
            copy.start()
            copies.append(copy)
    x = jnp.concatenate([xa_ref[...], xb_ref[...]], axis=0)
    for c in range(steps):
        cols = slice(c * tile, (c + 1) * tile)
        copies[c].wait()
        first = jnp.dot(x, w1[:, :, cols].reshape(D, tile), preferred_element_type=F32)
        hidden[:, cols] = jax.nn.gelu(first, approximate=True).astype(BF16)
    for c in range(steps):
        cols = slice(c * tile, (c + 1) * tile)
        copies[steps + c].wait()
        out = jnp.dot(hidden[...], w2[:, :, cols].reshape(D, tile), preferred_element_type=F32)
        oa_ref[:, cols] = out[:n].astype(BF16)
        ob_ref[:, cols] = out[n:].astype(BF16)


def expert(xa, xb, *weights, tile=512):
    shape = xa.shape
    xa, xb = xa.reshape(-1, D), xb.reshape(-1, D)
    n = xa.shape[0]
    held = (D // SLICE, SLICE, D)
    pick = len(weights) == 1
    if not pick:
        weights = [w.reshape(held) for w in weights]
    ya, yb = pl.pallas_call(
        functools.partial(expert_kernel, pick, tile),
        out_shape=(jax.ShapeDtypeStruct((n, D), BF16),) * 2,
        in_specs=[VMEM, VMEM] + [pl.BlockSpec(memory_space=pl.ANY)] * len(weights),
        out_specs=(VMEM, VMEM),
        scratch_shapes=[
            pltpu.VMEM(held, BF16),
            pltpu.VMEM(held, BF16),
            pltpu.VMEM((2 * n, D), BF16),
            pltpu.SemaphoreType.DMA((2 * D // tile,)),
        ],
        compiler_params=params(mib=48),
        cost_estimate=pl.CostEstimate(
            flops=8 * n * D * D, bytes_accessed=11 << 20, transcendentals=2 * n * D
        ),
    )(xa, xb, *weights)
    return ya.reshape(shape), yb.reshape(shape)


def combine_kernel(blocks, *refs):
    g_ref, ys, outs = refs[0], refs[1:5], refs[5:]
    if 0 in blocks:
        res_ref, outs = outs[0], outs[1:]
    for i, block in enumerate(blocks):
        rows = jnp.concatenate([y[i] for y in ys], axis=0)
        total = jnp.dot(g_ref[i, :, :TOK], rows, preferred_element_type=F32)
        total = total + jnp.dot(g_ref[i, :, TOK:], rows, preferred_element_type=F32)
        if block == 0:
            total = total + res_ref[...]
        for c in range(CHAINS):
            out = outs[i * CHAINS + c]
            out[...] = total[:, c * D // CHAINS : (c + 1) * D // CHAINS].astype(out.dtype)


def combine(blocks, gates, ys, *resid):
    shapes = [
        jax.ShapeDtypeStruct((TOK, D // CHAINS), F32 if i == 0 else BF16)
        for i in blocks
        for _ in range(CHAINS)
    ]
    outs = pl.pallas_call(
        functools.partial(combine_kernel, blocks),
        out_shape=shapes,
        in_specs=[VMEM] * (5 + len(resid)),
        out_specs=[VMEM] * len(shapes),
        compiler_params=params(),
        cost_estimate=pl.CostEstimate(
            flops=4 * len(blocks) * TOK * TOK * D, bytes_accessed=4 << 20, transcendentals=0
        ),
    )(gates, *ys, *resid)
    return [
        {block: outs[i * CHAINS + c] for i, block in enumerate(blocks)} for c in range(CHAINS)
    ]


def send(x, axis, n, shift):
    return lax.ppermute(x, axis, [(i, (i + shift) % n) for i in range(n)])


def after(x, *done):
    return lax.optimization_barrier((x,) + done)[0]


def ring_z(x):
    got = [x] + [None] * (NZ - 1)
    up, down = x, x
    for s in range(1, 4):
        up, down = send(up, "z", NZ, 1), send(down, "z", NZ, -1)
        got[NZ - s], got[s] = up, down
    half = x.shape[0] // 2
    up, down = send(up[:half], "z", NZ, 1), send(down[half:], "z", NZ, -1)
    got[4] = jnp.concatenate([up, down], axis=0)
    return got


def in_order(blocks):
    z = lax.axis_index("z")
    out = jnp.zeros((NZ,) + blocks[0].shape, blocks[0].dtype)
    for r, block in enumerate(blocks):
        out = lax.dynamic_update_slice(out, block[None], ((z + r) % NZ, 0, 0))
    return out


def add(a, b):
    return (a.astype(F32) + b.astype(F32)).astype(BF16)


def scatter_first(parts):
    half = TOK // 2
    down, up = send(parts[4][:half], "z", NZ, -1), send(parts[4][half:], "z", NZ, 1)
    down = jnp.concatenate([add(parts[5][:half], down), parts[5][half:]], axis=0)
    up = jnp.concatenate([parts[3][:half], add(parts[3][half:], up)], axis=0)
    return lax.optimization_barrier((down, up))


def scatter_rest(parts, down, up):
    for s in (6, 7):
        down, up = send(down, "z", NZ, -1), send(up, "z", NZ, 1)
        down, up = add(parts[s], down), add(parts[NZ - s], up)
    down, up = send(down, "z", NZ, -1), send(up, "z", NZ, 1)
    return (parts[0] + down.astype(F32) + up.astype(F32)).astype(BF16)


def per_device(
    hidden_in, queries, fresh_kv, stale_kv, modulation, w_out, router, fc_in, fc_out, expert_ids
):
    y, z = lax.axis_index("y"), lax.axis_index("z")
    pos = jnp.stack([y, z]).astype(jnp.int32)
    batch = lax.axis_size("batch")

    rows = D // batch
    w1, w2 = fc_in[0], fc_out[0]
    at = lax.axis_index("batch") * rows
    part = jnp.concatenate(
        [lax.dynamic_slice_in_dim(w, at, rows, 0) for w in (w1, w2)], axis=0
    )
    pieces, rest = [], router
    for _ in range(3):
        piece = lax.reduce_precision(rest, exponent_bits=8, mantissa_bits=7)
        rest = rest - piece
        pieces.append(piece.astype(BF16))
    router3 = jnp.pad(jnp.concatenate(pieces, axis=1), ((0, 0), (0, TOK - 3 * EXPERTS)))

    ids = jnp.pad(expert_ids.astype(BF16), ((0, 0), (0, IDS - 2)))
    heads = split_heads(after(stale_kv, part), queries, fresh_kv, ids)
    row = lax.all_to_all(heads, "z", split_axis=0, concat_axis=0, tiled=True)
    row, part_next, router3 = lax.optimization_barrier((row, send(part, "y", NY, -1), router3))
    hid = lax.all_gather(hidden_in, "z", axis=0, tiled=False)
    kv = row[:, : 2 * HEAD]
    kv_prev, kv_next = send(kv, "y", NY, 1), send(kv, "y", NY, -1)
    q, state = attend_own_row(row)
    kv_far = [send(after(kv_prev, q)[:4], "y", NY, 1), send(after(kv_next, q)[4:], "y", NY, -1)]
    w_next = lax.all_gather(after(part_next, q), "batch", axis=0, tiled=False)
    w_next = w_next.reshape(batch, 2, rows, D)
    state = attend_other_rows([kv_prev, kv_next], q, state, False)
    att = attend_other_rows(kv_far, q, state, True)
    att = in_order(ring_z(att)).reshape(HD, ROW)

    groups = []
    for blocks in (FAR, NEAR):
        x0, x1, x2, x3, gates, *own = norm_and_dispatch(
            blocks, pos, hid, att, w_out, modulation, router3, row
        )
        att = after(att, x2)
        groups.append((blocks, x0, x1, send(x2, "y", NY, 1), send(x3, "y", NY, -1), gates, own))
    attended = own[1]

    ys, last = [], ()
    for _, x0, x1, x_prev, x_next, _, _ in groups:
        y0, y3 = expert(after(x0, *last), x_next, w1, w2)
        y1, y2 = expert(after(x1, y0), x_prev, w_next)
        ys.append((y0, y1, send(y2, "y", NY, -1), send(y3, "y", NY, 1)))
        last = (y1,)
    (_, *_, far_gates, _), (_, *_, near_gates, own) = groups
    far = combine(FAR, after(far_gates, *last), ys[0])
    sums = [scatter_first(parts) for parts in far]
    near = combine(NEAR, after(near_gates, *sums[0], *sums[1]), ys[1], own[0])
    mixed = [scatter_rest(far[c] | near[c], *sums[c]) for c in range(CHAINS)]
    return attended, jnp.concatenate(mixed, axis=1)


def solution(mesh):
    split = Mesh(mesh.devices.reshape(NY, NZ, -1), ("y", "z", "batch"))
    tokens = P(("batch", "y", "z"), None)
    return jax.shard_map(
        per_device,
        mesh=split,
        in_specs=(
            tokens,
            tokens,
            tokens,
            tokens,
            P("batch", None),
            P(),
            P(),
            P(("y", "z"), None, None),
            P(("y", "z"), None, None),
            tokens,
        ),
        out_specs=(tokens, tokens),
        check_vma=False,
    )
```
